32 devices in a mesh: chan: 8 (over y, x, core), beam: 4 (over z).
Axes of the slice: x: 2, y: 2, z: 4, core: 2. Of those that a mesh axis runs over, the one named last changes fastest.
Arguments:
- images: float32 [256, 36, 128, 128], P('chan', 'beam')
- beam_weight: float32 [36, 128, 128], P('beam'), may hold values from 0.2 to 1
- offsets: int32 [36, 2], P('beam'), may hold values from 0 to 384, as said below
- rejected_indicator: int32 [256, 192, 512], P('chan', None, 'beam'), may hold values 0 or 1
- regression_indicator: int32 [256], replicated, may hold values 0 or 1
Outputs:
- cleaned_cube: float32 [256, 192, 512], P(None, 'chan', 'beam')
The draws below stay inside these ranges and needn't reach their ends.
Inputs may be any that keep to these rules, and one draw needn't show every extreme that they name: `offsets`: beam b = 6 r + q sits near row r * 64 // 5 and column q * 384 // 5, within 16; every sky pixel is covered by some beam; the first and last row and column of beams lie at the field's edges.
All inputs are finite; a program needn't handle non-finite values. No bound on the sum of `rejected_indicator` on one device may be relied on, other than what follows from the above.
Results may differ from the reference program's by a relative error of at most 0.00023.
Values sent between devices are 32-bit elements; how exact they have to be, the bound alone decides.
A program may use at most 128 MiB of HBM per device.

```python
import jax
import jax.numpy as jnp
from jax import lax

CHANNELS = 256
BEAMS = 36
BSIDE = 128
MOS_ROWS = 192
MOS_COLS = 512


def draw_images(key, part):
    first_key = jax.random.fold_in(key, 101)
    second_key = jax.random.fold_in(key, 202)
    position = (2.0 * jnp.arange(CHANNELS).astype(jnp.float32) + 1.0) / CHANNELS - 1.0
    square = position * position
    shape = (CHANNELS, BEAMS, BSIDE, BSIDE)
    coefficients = jax.random.normal(first_key, (4, BEAMS, BSIDE, BSIDE), jnp.float32)
    noise = jax.random.normal(second_key, shape, jnp.float32)
    scales = (3.0, 1.5, 1.0, 0.7)
    cube = noise + scales[0] * coefficients[0][None]
    cube = cube + scales[1] * position[:, None, None, None] * coefficients[1][None]
    cube = cube + (0.5 * (3.0 * square - 1.0))[:, None, None, None] * coefficients[2][None]
    cube = cube + scales[3] * (0.5 * (5.0 * square * position - 3.0 * position))[:, None, None, None] * coefficients[3][None]
    return cube.astype(jnp.float32)


def draw_offsets(key, part):
    row_key = jax.random.fold_in(key, 303)
    col_key = jax.random.fold_in(key, 404)
    jitter_span = BSIDE // 8
    index = jnp.arange(BEAMS, dtype=jnp.int32)
    grid_row = index // 6
    grid_col = index % 6
    base_row = grid_row * (MOS_ROWS - BSIDE) // 5
    base_col = grid_col * (MOS_COLS - BSIDE) // 5
    row_jitter = jax.random.randint(row_key, (BEAMS,), -jitter_span, jitter_span + 1, jnp.int32)
    col_jitter = jax.random.randint(col_key, (BEAMS,), -jitter_span, jitter_span + 1, jnp.int32)
    row_inner = jnp.logical_and(grid_row > 0, grid_row < 5).astype(jnp.int32)
    col_inner = jnp.logical_and(grid_col > 0, grid_col < 5).astype(jnp.int32)
    row_start = jnp.clip(base_row + row_inner * row_jitter, 0, MOS_ROWS - BSIDE)
    col_start = jnp.clip(base_col + col_inner * col_jitter, 0, MOS_COLS - BSIDE)
    return jnp.stack([row_start, col_start], axis=1).astype(jnp.int32)


def set_ends(values, key, least, largest):
    longest = values.shape.index(max(values.shape))
    spots = []
    for shift in (0, 1):
        where = [jax.random.randint(jax.random.fold_in(key, axis), (), 0, length) for axis, length in enumerate(values.shape)]
        where[longest] = (where[longest] + shift) % values.shape[longest]
        spots.append(tuple(where))
    return values.at[spots[0]].set(least).at[spots[1]].set(largest)


def levels(rng, shape, shards, least, top_value):
    level, own = 1.0, jax.random.fold_in(rng, 6)
    for axis_at, parts in shards:
        draws = jnp.exp(jax.random.uniform(jax.random.fold_in(own, axis_at), (parts,), jnp.float32, least / len(shards), top_value / len(shards)))
        level = level * jnp.repeat(draws, shape[axis_at] // parts).reshape([-1 if axis == axis_at else 1 for axis in range(len(shape))])
    return level


def setup_inputs(seed: int = 0) -> dict:
    keys = jax.random.split(jax.random.key(seed), 6)
    return {
        "images": draw_images(jax.random.fold_in(keys[5], 71), 0),
        "beam_weight": jnp.clip(0.2 + 0.8 * jax.random.uniform(keys[1], (BEAMS, BSIDE, BSIDE), jnp.float32) ** levels(keys[1], (BEAMS, BSIDE, BSIDE), ((0, 4),), -0.2, 0.2), 0.2, 1.0),
        "offsets": draw_offsets(jax.random.fold_in(keys[5], 71), 0),
        "rejected_indicator": set_ends((jax.random.randint(keys[3], (CHANNELS, MOS_ROWS, MOS_COLS), 0, 8) < 1).astype(jnp.int32), jax.random.fold_in(keys[3], 1), 0, 1),
        "regression_indicator": set_ends((jax.random.randint(keys[4], (CHANNELS,), 0, 4) < 3).astype(jnp.int32), jax.random.fold_in(keys[4], 1), 0, 1),
    }


def legendre(count):
    position = (2.0 * jnp.arange(count).astype(jnp.float32) + 1.0) / count - 1.0
    square = position * position
    return jnp.stack([jnp.ones_like(position), position, 0.5 * (3.0 * square - 1.0), 0.5 * (5.0 * square * position - 3.0 * position)], axis=1)

def solve_cubic(normal_matrix, right_side):
    factor = {}
    for outer in range(4):
        for inner in range(outer + 1):
            value = normal_matrix[outer * 4 + inner]
            for other in range(inner):
                value = value - factor[outer, other] * factor[inner, other]
            if outer == inner:
                factor[outer, outer] = jnp.sqrt(value)
            else:
                factor[outer, inner] = value / factor[inner, inner]
    forward = []
    for outer in range(4):
        value = right_side[outer]
        for other in range(outer):
            value = value - factor[outer, other] * forward[other]
        forward.append(value / factor[outer, outer])
    backward = [None] * 4
    for outer in range(3, -1, -1):
        value = forward[outer]
        for other in range(outer + 1, 4):
            value = value - factor[other, outer] * backward[other]
        backward[outer] = value / factor[outer, outer]
    return jnp.stack(backward, axis=0)

def clean_tiles(celestial_image, importance_factor):
    table = legendre(celestial_image.shape[0])
    products = jnp.stack([table[:, outer] * table[:, inner] for outer in range(4) for inner in range(4)], axis=0)
    normal_matrix = jnp.dot(products, importance_factor, precision=lax.Precision.HIGHEST, preferred_element_type=jnp.float32)
    right_side = jnp.dot(table.T, importance_factor * celestial_image, precision=lax.Precision.HIGHEST, preferred_element_type=jnp.float32)
    coefficients = solve_cubic(normal_matrix, right_side)
    continuum = jnp.dot(table, coefficients, precision=lax.Precision.HIGHEST, preferred_element_type=jnp.float32)
    residual = celestial_image - continuum
    padded = jnp.pad(residual, ((1, 1), (0, 0)))
    return 0.25 * padded[:-2] + 0.5 * residual + 0.25 * padded[2:]

def reference(images, beam_weight, offsets, rejected_indicator, regression_indicator):
    exponent = 1.0 + 0.5 * jnp.arange(CHANNELS).astype(jnp.float32) / (CHANNELS - 1)
    side = images.shape[2]

    def place(index, state_pair):
        dividend_accumulator, normalizer_accumulated = state_pair
        beam_image = lax.dynamic_index_in_dim(images, index, 1, keepdims=False)
        log_weight = jnp.log(lax.dynamic_index_in_dim(beam_weight, index, 0, keepdims=False))
        response = jnp.exp(exponent[:, None, None] * log_weight[None])
        corner = (jnp.zeros((), jnp.int32), offsets[index, 0].astype(jnp.int32), offsets[index, 1].astype(jnp.int32))
        extent = (CHANNELS, side, side)
        dividend_accumulator = lax.dynamic_update_slice(dividend_accumulator, lax.dynamic_slice(dividend_accumulator, corner, extent) + response * beam_image, corner)
        normalizer_accumulated = lax.dynamic_update_slice(normalizer_accumulated, lax.dynamic_slice(normalizer_accumulated, corner, extent) + response * response, corner)
        return (dividend_accumulator, normalizer_accumulated)
    empty = jnp.zeros((CHANNELS, MOS_ROWS, MOS_COLS), jnp.float32)
    dividend_accumulator, normalizer_accumulated = lax.fori_loop(0, BEAMS, place, (empty, empty))
    accepted_entries = 1.0 - rejected_indicator.astype(jnp.float32)
    celestial_image = accepted_entries * dividend_accumulator / normalizer_accumulated
    importance_factor = normalizer_accumulated * (regression_indicator.astype(jnp.float32)[:, None, None] * accepted_entries + 0.01)
    flat_sky = celestial_image.reshape(CHANNELS, MOS_ROWS * MOS_COLS)
    flat_weight = importance_factor.reshape(CHANNELS, MOS_ROWS * MOS_COLS)
    return clean_tiles(flat_sky, flat_weight).reshape(CHANNELS, MOS_ROWS, MOS_COLS)
```

```python
import functools

import jax
import jax.numpy as jnp
from jax import lax
from jax.experimental import pallas as pl
from jax.experimental.pallas import tpu as pltpu
from jax.sharding import PartitionSpec as P

MOS_ROWS = 192
MOS_COLS = 512
GRID = 6
JITTER = 16
LANES = 128
OUTSIDE = -1.0e4
MESH = pl.DeviceIdType.MESH


def start_range(position, span):
    if position == 0:
        return 0, 0
    if position == GRID - 1:
        return span, span
    middle = position * span // (GRID - 1)
    return max(0, middle - JITTER), min(span, middle + JITTER)


def covered_rows(group, beams_each, side, block):
    first, last = MOS_ROWS, 0
    for beam in range(group * beams_each, (group + 1) * beams_each):
        low, high = start_range(beam % GRID, MOS_COLS - side)
        if high + side <= block * LANES or low >= (block + 1) * LANES:
            continue
        low, high = start_range(beam // GRID, MOS_ROWS - side)
        first, last = min(first, low), max(last, high + side)
    return first // 8 * 8, min(MOS_ROWS, -(-last // 8) * 8)


def place_kernel(
    where_ref, offsets_ref, image_ref, weight_ref, sums_ref, tiles_ref, log_ref, plane_ref, *, slope
):
    step = pl.program_id(0)
    blocks, depth, _, _ = sums_ref.shape
    beams, side, _ = weight_ref.shape
    tile_rows = tiles_ref.shape[2]
    piece = 32
    lane = lax.broadcasted_iota(jnp.int32, (piece, LANES), 1)

    def corner(beam):
        row, col = offsets_ref[beam, 0], offsets_ref[beam, 1]
        return row, lax.shift_right_logical(col, 7), jnp.bitwise_and(col, LANES - 1)

    @pl.when(step == 0)
    def _():
        log_ref[...] = jnp.log(weight_ref[...])

        def spread(beam, carry):
            row, block, shift = corner(beam)
            plane_ref[...] = jnp.full(plane_ref.shape, OUTSIDE, jnp.float32)

            def part(index, inner):
                start = pl.multiple_of(index * piece, piece)
                value = pltpu.roll(log_ref[beam, pl.ds(start, piece), :], shift, 1)
                plane_ref[block, pl.ds(row + start, piece), :] = jnp.where(
                    lane >= shift, value, OUTSIDE
                )

                @pl.when(block < blocks - 1)
                def _():
                    plane_ref[block + 1, pl.ds(row + start, piece), :] = jnp.where(
                        lane < shift, value, OUTSIDE
                    )

                return inner

            lax.fori_loop(0, side // piece, part, 0)
            tiles_ref[:, beam, :, :] = plane_ref[:, pl.ds(where_ref[1], tile_rows), :]
            return carry

        lax.fori_loop(0, beams, spread, 0)

    sums_ref[...] = jnp.zeros(sums_ref.shape, jnp.float32)
    exponent = 1.0 + slope * (where_ref[0] + step * depth).astype(jnp.float32)

    def add_beam(beam, carry):
        row, block, shift = corner(beam)
        after = jnp.minimum(block + 1, blocks - 1)

        def part(index, inner):
            start = pl.multiple_of(index * piece, piece)
            rows = pl.ds(row + start, piece)
            logs = log_ref[beam, pl.ds(start, piece), :]
            response = jnp.exp(exponent * logs)
            ratio = jnp.exp(slope * logs)
            for channel in range(depth):
                value = image_ref[channel, beam, pl.ds(start, piece), :] * response
                value = pltpu.roll(value, shift, 1)
                sums_ref[block, channel, rows, :] += jnp.where(lane >= shift, value, 0.0)
                sums_ref[after, channel, rows, :] += jnp.where(lane < shift, value, 0.0)
                response = response * ratio
            return inner

        lax.fori_loop(0, side // piece, part, 0)
        return carry

    lax.fori_loop(0, beams, add_beam, 0)


def place(where, offsets, images, beam_weight, blocks, tile_rows, channels):
    ch_dev, beams, side, _ = images.shape
    depth = 4
    return pl.pallas_call(
        functools.partial(place_kernel, slope=0.5 / (channels - 1)),
        grid=(ch_dev // depth,),
        in_specs=[
            pl.BlockSpec(memory_space=pltpu.SMEM),
            pl.BlockSpec(memory_space=pltpu.SMEM),
            pl.BlockSpec((depth, beams, side, side), lambda s: (s, 0, 0, 0)),
            pl.BlockSpec((beams, side, side), lambda s: (0, 0, 0)),
        ],
        out_specs=[
            pl.BlockSpec((blocks, depth, MOS_ROWS, LANES), lambda s: (0, s, 0, 0)),
            pl.BlockSpec((blocks, beams, tile_rows, LANES), lambda s: (0, 0, 0, 0)),
        ],
        out_shape=[
            jax.ShapeDtypeStruct((blocks, ch_dev, MOS_ROWS, LANES), jnp.float32),
            jax.ShapeDtypeStruct((blocks, beams, tile_rows, LANES), jnp.float32),
        ],
        scratch_shapes=[
            pltpu.VMEM((beams, side, side), jnp.float32),
            pltpu.VMEM((blocks, MOS_ROWS, LANES), jnp.float32),
        ],
        compiler_params=pltpu.CompilerParams(vmem_limit_bytes=48 << 20),
        name="place_beams",
    )(where, offsets, images, beam_weight)


def exchange_kernel(
    sums_ref,
    flags_ref,
    logs_ref,
    sky_out,
    flag_out,
    log_out,
    own,
    up,
    down,
    rowed,
    own_sem,
    keep_sem,
    up_recv,
    down_recv,
    up_send,
    down_send,
    sky_send,
    sky_recv,
    flag_send,
    flag_recv,
    log_send,
    log_recv,
    *,
    groups,
    tiles,
    depth,
    reach_up,
    reach_down,
):
    group = lax.axis_index("beam")
    tile = lax.axis_index("chan")
    ch_dev = sums_ref.shape[1]
    tile_rows = flags_ref.shape[2]
    beams = logs_ref.shape[1]
    steps = ch_dev // depth

    others = [lax.rem(tile + k, tiles) for k in range(1, tiles)]
    columns = [lax.rem(group + k, groups) for k in range(1, groups)]

    barrier = pltpu.get_barrier_semaphore()
    for other in others:
        pl.semaphore_signal(barrier, inc=1, device_id={"chan": other}, device_id_type=MESH)
    for other in columns:
        pl.semaphore_signal(barrier, inc=1, device_id={"beam": other}, device_id_type=MESH)

    def load(step):
        span = pl.ds(step * depth, depth)
        return pltpu.make_async_copy(sums_ref.at[:, span], own.at[:, span], own_sem.at[step])

    def fetch(step, carry):
        load(step).start()
        return carry

    lax.fori_loop(0, steps, fetch, 0)
    mine = pl.ds(tile * ch_dev, ch_dev)
    kept = [
        pltpu.make_async_copy(flags_ref.at[:, tile], flag_out.at[mine], keep_sem.at[0]),
        pltpu.make_async_copy(
            logs_ref.at[group], log_out.at[pl.ds(group * beams, beams)], keep_sem.at[1]
        ),
    ]
    for copy in kept:
        copy.start()
    pl.semaphore_wait(barrier, len(others) + len(columns))

    small = []
    for k, other in enumerate(columns):
        small.append(
            pltpu.make_async_remote_copy(
                src_ref=logs_ref.at[other],
                dst_ref=log_out.at[pl.ds(group * beams, beams)],
                send_sem=log_send.at[k],
                recv_sem=log_recv.at[k],
                device_id={"beam": other},
                device_id_type=MESH,
            )
        )
    for k, other in enumerate(others):
        small.append(
            pltpu.make_async_remote_copy(
                src_ref=flags_ref.at[:, other],
                dst_ref=flag_out.at[mine],
                send_sem=flag_send.at[k],
                recv_sem=flag_recv.at[k],
                device_id={"chan": other},
                device_id_type=MESH,
            )
        )
    for copy in small:
        copy.start()

    def up_copy(z, block, step):
        span, rows = pl.ds(step * depth, depth), pl.ds(0, reach_up[z, block])
        source = own.at[block, span, rows] if z == 0 else up.at[block - 1, span, rows]
        return pltpu.make_async_remote_copy(
            src_ref=source,
            dst_ref=up.at[block - 1, span, rows],
            send_sem=up_send.at[block],
            recv_sem=up_recv.at[step, block],
            device_id={"beam": z + 1},
            device_id_type=MESH,
        )

    def down_copy(z, block, step):
        first = reach_down[z, block]
        span, rows = pl.ds(step * depth, depth), pl.ds(first, MOS_ROWS - first)
        source = own.at[block, span, rows] if z == groups - 1 else down.at[block, span, rows]
        return pltpu.make_async_remote_copy(
            src_ref=source,
            dst_ref=down.at[block, span, rows],
            send_sem=down_send.at[block],
            recv_sem=down_recv.at[step, block],
            device_id={"beam": z - 1},
            device_id_type=MESH,
        )

    def sky_copy(k, other, span):
        return pltpu.make_async_remote_copy(
            src_ref=rowed.at[other, span],
            dst_ref=sky_out.at[pl.ds(tile * ch_dev + span.start, span.size)],
            send_sem=sky_send.at[k],
            recv_sem=sky_recv.at[k],
            device_id={"chan": other},
            device_id_type=MESH,
        )

    for z in range(groups):

        @pl.when(group == z)
        def _(z=z):
            def work(step, carry):
                span = pl.ds(step * depth, depth)
                load(step).wait()
                for block in range(groups - 1, z, -1):
                    if z > 0:
                        old, new = reach_up[z - 1, block], reach_up[z, block]
                        up_copy(z - 1, block, step).wait_recv()
                        up[block - 1, span, 0:old, :] += own[block, span, 0:old, :]
                        if new > old:
                            up[block - 1, span, old:new, :] = own[block, span, old:new, :]
                    up_copy(z, block, step).start()
                for block in range(z):
                    if z < groups - 1:
                        old, new = reach_down[z + 1, block], reach_down[z, block]
                        down_copy(z + 1, block, step).wait_recv()
                        down[block, span, old:, :] += own[block, span, old:, :]
                        if new < old:
                            down[block, span, new:old, :] = own[block, span, new:old, :]
                    down_copy(z, block, step).start()
                if z > 0:
                    old = reach_up[z - 1, z]
                    up_copy(z - 1, z, step).wait_recv()
                    own[z, span, 0:old, :] += up[z - 1, span, 0:old, :]
                if z < groups - 1:
                    old = reach_down[z + 1, z]
                    down_copy(z + 1, z, step).wait_recv()
                    own[z, span, old:, :] += down[z, span, old:, :]
                for index in range(tiles):
                    rowed[index, span, :, :] = own[
                        z, span, index * tile_rows : (index + 1) * tile_rows, :
                    ]
                for k, other in enumerate(others):
                    sky_copy(k, other, span).start()
                return carry

            lax.fori_loop(0, steps, work, 0)
            for block in range(z + 1, groups):
                ref = up.at[block - 1, :, pl.ds(0, reach_up[z, block])]
                pltpu.make_async_copy(ref, ref, up_send.at[block]).wait()
            for block in range(z):
                first = reach_down[z, block]
                ref = down.at[block, :, pl.ds(first, MOS_ROWS - first)]
                pltpu.make_async_copy(ref, ref, down_send.at[block]).wait()

    kept.append(pltpu.make_async_copy(rowed.at[tile], sky_out.at[mine], keep_sem.at[2]))
    kept[-1].start()
    for copy in small:
        copy.wait()
    for k, other in enumerate(others):
        sky_copy(k, other, pl.ds(0, ch_dev)).wait()
    for copy in kept:
        copy.wait()


def exchange(sums, flags, logs, groups, tiles):
    ch_dev = sums.shape[1]
    tile_rows = flags.shape[2]
    beams = logs.shape[1]
    depth = 2
    steps = ch_dev // depth
    side = MOS_ROWS - start_range(GRID - 1, MOS_ROWS - LANES)[0]
    reach_up, reach_down = {}, {}
    for block in range(groups):
        rows = [covered_rows(group, beams, side, block) for group in range(groups)]
        for z in range(groups):
            reach_up[z, block] = max(high for _, high in rows[: z + 1])
            reach_down[z, block] = min(low for low, _ in rows[z:])
    dma = pltpu.SemaphoreType.DMA
    any_space = pl.BlockSpec(memory_space=pl.ANY)
    return pl.pallas_call(
        functools.partial(
            exchange_kernel,
            groups=groups,
            tiles=tiles,
            depth=depth,
            reach_up=reach_up,
            reach_down=reach_down,
        ),
        in_specs=[any_space] * 3,
        out_specs=[any_space] * 3,
        out_shape=[
            jax.ShapeDtypeStruct((tiles * ch_dev, tile_rows, LANES), jnp.float32),
            jax.ShapeDtypeStruct((tiles * ch_dev, tile_rows, LANES), jnp.int32),
            jax.ShapeDtypeStruct((groups * beams, tile_rows, LANES), jnp.float32),
        ],
        scratch_shapes=[
            pltpu.VMEM((groups, ch_dev, MOS_ROWS, LANES), jnp.float32),
            pltpu.VMEM((groups - 1, ch_dev, MOS_ROWS, LANES), jnp.float32),
            pltpu.VMEM((groups - 1, ch_dev, MOS_ROWS, LANES), jnp.float32),
            pltpu.VMEM((tiles, ch_dev, tile_rows, LANES), jnp.float32),
            dma((steps,)),
            dma((3,)),
            dma((steps, groups)),
            dma((steps, groups)),
            dma((groups,)),
            dma((groups,)),
            dma((tiles - 1,)),
            dma((tiles - 1,)),
            dma((tiles - 1,)),
            dma((tiles - 1,)),
            dma((groups - 1,)),
            dma((groups - 1,)),
        ],
        compiler_params=pltpu.CompilerParams(
            collective_id=0, has_side_effects=True, vmem_limit_bytes=56 << 20
        ),
        name="exchange",
    )(sums, flags, logs)


def solve_cubic(normal_matrix, right_side):
    factor = {}
    for outer in range(4):
        for inner in range(outer + 1):
            value = normal_matrix[outer, inner]
            for other in range(inner):
                value = value - factor[outer, other] * factor[inner, other]
            if outer == inner:
                factor[outer, outer] = jnp.sqrt(value)
            else:
                factor[outer, inner] = value / factor[inner, inner]
    forward = []
    for outer in range(4):
        value = right_side[outer]
        for other in range(outer):
            value = value - factor[outer, other] * forward[other]
        forward.append(value / factor[outer, outer])
    backward = [None] * 4
    for outer in range(3, -1, -1):
        value = forward[outer]
        for other in range(outer + 1, 4):
            value = value - factor[other, outer] * backward[other]
        backward[outer] = value / factor[outer, outer]
    return backward


POLYNOMIALS = (
    {0: 1.0},
    {1: 1.0},
    {0: -0.5, 2: 1.5},
    {1: -1.5, 3: 2.5},
)


def fit_kernel(where_ref, regression_ref, sky_ref, flag_ref, log_ref, out_ref, total_ref, *, slope):
    channels, rows, _ = sky_ref.shape
    piece = 8 if rows % 8 == 0 else rows
    run = 16
    first = where_ref[0]
    beams = [(r * GRID, q) for r in range(GRID) for q in range(3)]

    def totals(index, carry):
        start = index * run
        exponent = 1.0 + slope * start.astype(jnp.float32)
        for part in range(rows // piece):
            span = pl.ds(part * piece, piece)
            total = [jnp.zeros((piece, LANES), jnp.float32)] * run
            for begin, q in beams:
                logs = log_ref[begin + q + first, span, :]
                value = jnp.exp((2.0 * exponent) * logs)
                ratio = jnp.exp((2.0 * slope) * logs)
                for k in range(run):
                    total[k] = total[k] + value
                    if k < run - 1:
                        value = value * ratio
            for k in range(run):
                total_ref[start + k, span, :] = total[k]
        return carry

    lax.fori_loop(0, channels // run, totals, 0)

    def position(channel):
        return (2.0 * channel.astype(jnp.float32) + 1.0) * (1.0 / channels) - 1.0

    def gather(channel, carry):
        powers, rights = list(carry[:7]), list(carry[7:])
        x = position(channel)
        open_sky = 1.0 - flag_ref[channel].astype(jnp.float32)
        total = total_ref[channel]
        sky = open_sky * sky_ref[channel] / total
        total_ref[channel] = sky
        chosen = regression_ref[channel].astype(jnp.float32)
        weight = total * (chosen * open_sky + 0.01)
        right = weight * sky
        for k in range(7):
            powers[k] = powers[k] + weight
            if k < 6:
                weight = weight * x
        for k in range(4):
            rights[k] = rights[k] + right
            if k < 3:
                right = right * x
        return tuple(powers) + tuple(rights)

    zero = jnp.zeros((rows, LANES), jnp.float32)
    sums = lax.fori_loop(0, channels, gather, (zero,) * 11, unroll=4)
    powers, rights = sums[:7], sums[7:]
    normal = {}
    for outer in range(4):
        for inner in range(outer + 1):
            terms = {}
            for a, u in POLYNOMIALS[outer].items():
                for b, v in POLYNOMIALS[inner].items():
                    terms[a + b] = terms.get(a + b, 0.0) + u * v
            normal[outer, inner] = sum(v * powers[k] for k, v in terms.items())
    right_side = [sum(v * rights[k] for k, v in POLYNOMIALS[o].items()) for o in range(4)]
    fitted = solve_cubic(normal, right_side)

    def residual(channel):
        x = position(channel)
        square = x * x
        continuum = (
            fitted[0]
            + x * fitted[1]
            + (0.5 * (3.0 * square - 1.0)) * fitted[2]
            + (0.5 * (5.0 * square * x - 3.0 * x)) * fitted[3]
        )
        return total_ref[channel] - continuum

    def smooth(channel, carry):
        before, here = carry
        after = residual(channel + 1)
        out_ref[channel] = 0.25 * before + 0.5 * here + 0.25 * after
        return here, after

    before, here = lax.fori_loop(
        0, channels - 1, smooth, (zero, residual(jnp.int32(0))), unroll=3
    )
    out_ref[channels - 1] = 0.25 * before + 0.5 * here


def fit(where, regression, sky, flags, logs):
    channels = sky.shape[0]
    smem = pl.BlockSpec(memory_space=pltpu.SMEM)
    vmem = pl.BlockSpec(memory_space=pltpu.VMEM)
    return pl.pallas_call(
        functools.partial(fit_kernel, slope=0.5 / (channels - 1)),
        in_specs=[smem, smem, vmem, vmem, vmem],
        out_specs=vmem,
        out_shape=jax.ShapeDtypeStruct(sky.shape, jnp.float32),
        scratch_shapes=[pltpu.VMEM(sky.shape, jnp.float32)],
        compiler_params=pltpu.CompilerParams(vmem_limit_bytes=48 << 20),
        name="fit",
    )(where, regression, sky, flags, logs)


def local(
    images, beam_weight, offsets, rejected_indicator, regression_indicator, *, groups, tiles
):
    ch_dev = images.shape[0]
    channels = regression_indicator.shape[0]
    tile_rows = MOS_ROWS // tiles
    tile = lax.axis_index("chan")
    group = lax.axis_index("beam")
    where = jnp.stack([tile * ch_dev, tile * tile_rows]).astype(jnp.int32)
    sums, logs = place(where, offsets, images, beam_weight, groups, tile_rows, channels)
    flags = rejected_indicator.reshape(ch_dev, tiles, tile_rows, rejected_indicator.shape[2])
    sky, flags, logs = exchange(sums, flags, logs, groups, tiles)
    return fit(group[None].astype(jnp.int32), regression_indicator, sky, flags, logs)


def solution(mesh):
    in_specs = (
        P("chan", "beam", None, None),
        P("beam", None, None),
        P("beam", None),
        P("chan", None, "beam"),
        P(),
    )
    out_specs = P(None, "chan", "beam")
    body = functools.partial(local, groups=mesh.shape["beam"], tiles=mesh.shape["chan"])
    return jax.shard_map(body, mesh=mesh, in_specs=in_specs, out_specs=out_specs, check_vma=False)
```

```python
import functools

import jax
import jax.numpy as jnp
from jax import lax
from jax.experimental import pallas as pl
from jax.experimental.pallas import tpu as pltpu
from jax.sharding import PartitionSpec as P

MOS_ROWS = 192
MOS_COLS = 512
GRID = 6
JITTER = 16
LANES = 128
OUTSIDE = -1.0e4
MESH = pl.DeviceIdType.MESH


def start_range(position, span):
    if position == 0:
        return 0, 0
    if position == GRID - 1:
        return span, span
    middle = position * span // (GRID - 1)
    return max(0, middle - JITTER), min(span, middle + JITTER)


def covered_rows(group, beams_each, side, block):
    first, last = MOS_ROWS, 0
    for beam in range(group * beams_each, (group + 1) * beams_each):
        low, high = start_range(beam % GRID, MOS_COLS - side)
        if high + side <= block * LANES or low >= (block + 1) * LANES:
            continue
        low, high = start_range(beam // GRID, MOS_ROWS - side)
        first, last = min(first, low), max(last, high + side)
    return first // 8 * 8, min(MOS_ROWS, -(-last // 8) * 8)


def place_kernel(
    where_ref, offsets_ref, image_ref, weight_ref, sums_ref, tiles_ref, log_ref, plane_ref, *, slope
):
    step = pl.program_id(0)
    blocks, depth, _, _ = sums_ref.shape
    beams, side, _ = weight_ref.shape
    tile_rows = tiles_ref.shape[2]
    piece = 64
    lane = lax.broadcasted_iota(jnp.int32, (piece, LANES), 1)

    def corner(beam):
        row, col = offsets_ref[beam, 0], offsets_ref[beam, 1]
        return row, lax.shift_right_logical(col, 7), jnp.bitwise_and(col, LANES - 1)

    @pl.when(step == 0)
    def _():
        log_ref[...] = jnp.log(weight_ref[...])

        def spread(beam, carry):
            row, block, shift = corner(beam)
            plane_ref[...] = jnp.full(plane_ref.shape, OUTSIDE, jnp.float32)

            def part(index, inner):
                start = pl.multiple_of(index * piece, piece)
                value = pltpu.roll(log_ref[beam, pl.ds(start, piece), :], shift, 1)
                plane_ref[block, pl.ds(row + start, piece), :] = jnp.where(
                    lane >= shift, value, OUTSIDE
                )

                @pl.when(block < blocks - 1)
                def _():
                    plane_ref[block + 1, pl.ds(row + start, piece), :] = jnp.where(
                        lane < shift, value, OUTSIDE
                    )

                return inner

            lax.fori_loop(0, side // piece, part, 0)
            tiles_ref[:, beam, :, :] = plane_ref[:, pl.ds(where_ref[1], tile_rows), :]
            return carry

        lax.fori_loop(0, beams, spread, 0)

    sums_ref[...] = jnp.zeros(sums_ref.shape, jnp.float32)
    exponent = 1.0 + slope * (where_ref[0] + step * depth).astype(jnp.float32)

    def add_beam(beam, carry):
        row, block, shift = corner(beam)
        after = jnp.minimum(block + 1, blocks - 1)

        def part(index, inner):
            start = pl.multiple_of(index * piece, piece)
            rows = pl.ds(row + start, piece)
            logs = log_ref[beam, pl.ds(start, piece), :]
            response = jnp.exp(exponent * logs)
            ratio = jnp.exp(slope * logs)
            values = []
            for channel in range(depth):
                value = image_ref[channel, beam, pl.ds(start, piece), :] * response
                values.append(pltpu.roll(value, shift, 1))
                response = response * ratio
            for target, inside in ((block, lane >= shift), (after, lane < shift)):
                sums = [
                    sums_ref[target, channel, rows, :] + jnp.where(inside, value, 0.0)
                    for channel, value in enumerate(values)
                ]
                for channel, value in enumerate(sums):
                    sums_ref[target, channel, rows, :] = value
            return inner

        lax.fori_loop(0, side // piece, part, 0)
        return carry

    lax.fori_loop(0, beams, add_beam, 0)


def place(where, offsets, images, beam_weight, blocks, tile_rows, channels):
    ch_dev, beams, side, _ = images.shape
    depth = 4
    return pl.pallas_call(
        functools.partial(place_kernel, slope=0.5 / (channels - 1)),
        grid=(ch_dev // depth,),
        in_specs=[
            pl.BlockSpec(memory_space=pltpu.SMEM),
            pl.BlockSpec(memory_space=pltpu.SMEM),
            pl.BlockSpec((depth, beams, side, side), lambda s: (s, 0, 0, 0)),
            pl.BlockSpec((beams, side, side), lambda s: (0, 0, 0)),
        ],
        out_specs=[
            pl.BlockSpec((blocks, depth, MOS_ROWS, LANES), lambda s: (0, s, 0, 0)),
            pl.BlockSpec((blocks, beams, tile_rows, LANES), lambda s: (0, 0, 0, 0)),
        ],
        out_shape=[
            jax.ShapeDtypeStruct((blocks, ch_dev, MOS_ROWS, LANES), jnp.float32),
            jax.ShapeDtypeStruct((blocks, beams, tile_rows, LANES), jnp.float32),
        ],
        scratch_shapes=[
            pltpu.VMEM((beams, side, side), jnp.float32),
            pltpu.VMEM((blocks, MOS_ROWS, LANES), jnp.float32),
        ],
        compiler_params=pltpu.CompilerParams(vmem_limit_bytes=48 << 20),
        name="place_beams",
    )(where, offsets, images, beam_weight)


def exchange_kernel(
    sums_ref,
    flags_ref,
    logs_ref,
    sky_out,
    flag_out,
    log_out,
    own,
    up,
    down,
    rowed,
    own_sem,
    keep_sem,
    up_recv,
    down_recv,
    up_send,
    down_send,
    sky_send,
    sky_recv,
    flag_send,
    flag_recv,
    log_send,
    log_recv,
    *,
    groups,
    tiles,
    depth,
    reach_up,
    reach_down,
):
    group = lax.axis_index("beam")
    tile = lax.axis_index("chan")
    ch_dev = sums_ref.shape[1]
    tile_rows = flags_ref.shape[2]
    beams = logs_ref.shape[1]
    steps = ch_dev // depth

    others = [lax.rem(tile + k, tiles) for k in range(1, tiles)]
    columns = [lax.rem(group + k, groups) for k in range(1, groups)]

    barrier = pltpu.get_barrier_semaphore()
    for other in others:
        pl.semaphore_signal(barrier, inc=1, device_id={"chan": other}, device_id_type=MESH)
    for other in columns:
        pl.semaphore_signal(barrier, inc=1, device_id={"beam": other}, device_id_type=MESH)

    def load(step):
        span = pl.ds(step * depth, depth)
        return pltpu.make_async_copy(sums_ref.at[:, span], own.at[:, span], own_sem.at[step])

    def fetch(step, carry):
        load(step).start()
        return carry

    lax.fori_loop(0, steps, fetch, 0)
    mine = pl.ds(tile * ch_dev, ch_dev)
    kept = [
        pltpu.make_async_copy(flags_ref.at[:, tile], flag_out.at[mine], keep_sem.at[0]),
        pltpu.make_async_copy(
            logs_ref.at[group], log_out.at[pl.ds(group * beams, beams)], keep_sem.at[1]
        ),
    ]
    for copy in kept:
        copy.start()
    pl.semaphore_wait(barrier, len(others) + len(columns))

    small = []
    for k, other in enumerate(columns):
        small.append(
            pltpu.make_async_remote_copy(
                src_ref=logs_ref.at[other],
                dst_ref=log_out.at[pl.ds(group * beams, beams)],
                send_sem=log_send.at[k],
                recv_sem=log_recv.at[k],
                device_id={"beam": other},
                device_id_type=MESH,
            )
        )
    for k, other in enumerate(others):
        small.append(
            pltpu.make_async_remote_copy(
                src_ref=flags_ref.at[:, other],
                dst_ref=flag_out.at[mine],
                send_sem=flag_send.at[k],
                recv_sem=flag_recv.at[k],
                device_id={"chan": other},
                device_id_type=MESH,
            )
        )
    for copy in small:
        copy.start()

    def up_copy(z, block, step):
        span, rows = pl.ds(step * depth, depth), pl.ds(0, reach_up[z, block])
        source = own.at[block, span, rows] if z == 0 else up.at[block - 1, span, rows]
        return pltpu.make_async_remote_copy(
            src_ref=source,
            dst_ref=up.at[block - 1, span, rows],
            send_sem=up_send.at[block],
            recv_sem=up_recv.at[step, block],
            device_id={"beam": z + 1},
            device_id_type=MESH,
        )

    def down_copy(z, block, step):
        first = reach_down[z, block]
        span, rows = pl.ds(step * depth, depth), pl.ds(first, MOS_ROWS - first)
        source = own.at[block, span, rows] if z == groups - 1 else down.at[block, span, rows]
        return pltpu.make_async_remote_copy(
            src_ref=source,
            dst_ref=down.at[block, span, rows],
            send_sem=down_send.at[block],
            recv_sem=down_recv.at[step, block],
            device_id={"beam": z - 1},
            device_id_type=MESH,
        )

    def sky_copy(k, other, span):
        return pltpu.make_async_remote_copy(
            src_ref=rowed.at[other, span],
            dst_ref=sky_out.at[pl.ds(tile * ch_dev + span.start, span.size)],
            send_sem=sky_send.at[k],
            recv_sem=sky_recv.at[k],
            device_id={"chan": other},
            device_id_type=MESH,
        )

    for z in range(groups):

        @pl.when(group == z)
        def _(z=z):
            lower = 2 * z < groups
            up_lag, down_lag = (0, 2) if lower else (2, 0)
            last_lag = 6 if z in (0, groups - 1) else 3

            def pass_up(step):
                span = pl.ds(step * depth, depth)
                for block in range(groups - 1, z, -1):
                    if z > 0:
                        old, new = reach_up[z - 1, block], reach_up[z, block]
                        up_copy(z - 1, block, step).wait_recv()
                        up[block - 1, span, 0:old, :] += own[block, span, 0:old, :]
                        if new > old:
                            up[block - 1, span, old:new, :] = own[block, span, old:new, :]
                    up_copy(z, block, step).start()

            def pass_down(step):
                span = pl.ds(step * depth, depth)
                for block in range(z):
                    if z < groups - 1:
                        old, new = reach_down[z + 1, block], reach_down[z, block]
                        down_copy(z + 1, block, step).wait_recv()
                        down[block, span, old:, :] += own[block, span, old:, :]
                        if new < old:
                            down[block, span, new:old, :] = own[block, span, new:old, :]
                    down_copy(z, block, step).start()

            def finish(step):
                span = pl.ds(step * depth, depth)
                if z > 0:
                    old = reach_up[z - 1, z]
                    up_copy(z - 1, z, step).wait_recv()
                    own[z, span, 0:old, :] += up[z - 1, span, 0:old, :]
                if z < groups - 1:
                    old = reach_down[z + 1, z]
                    down_copy(z + 1, z, step).wait_recv()
                    own[z, span, old:, :] += down[z, span, old:, :]
                for index in range(tiles):
                    rowed[index, span, :, :] = own[
                        z, span, index * tile_rows : (index + 1) * tile_rows, :
                    ]
                for k, other in enumerate(others):
                    sky_copy(k, other, span).start()

            def work(turn, carry):
                @pl.when(turn < steps)
                def _():
                    load(turn).wait()

                for lag, act in ((up_lag, pass_up), (down_lag, pass_down), (last_lag, finish)):

                    @pl.when(jnp.logical_and(turn >= lag, turn < steps + lag))
                    def _(lag=lag, act=act):
                        act(turn - lag)

                return carry

            lax.fori_loop(0, steps + last_lag, work, 0)
            for block in range(z + 1, groups):
                ref = up.at[block - 1, :, pl.ds(0, reach_up[z, block])]
                pltpu.make_async_copy(ref, ref, up_send.at[block]).wait()
            for block in range(z):
                first = reach_down[z, block]
                ref = down.at[block, :, pl.ds(first, MOS_ROWS - first)]
                pltpu.make_async_copy(ref, ref, down_send.at[block]).wait()

    kept.append(pltpu.make_async_copy(rowed.at[tile], sky_out.at[mine], keep_sem.at[2]))
    kept[-1].start()
    for copy in small:
        copy.wait()
    for k, other in enumerate(others):
        sky_copy(k, other, pl.ds(0, ch_dev)).wait()
    for copy in kept:
        copy.wait()


def exchange(sums, flags, logs, groups, tiles):
    ch_dev = sums.shape[1]
    tile_rows = flags.shape[2]
    beams = logs.shape[1]
    depth = 2
    steps = ch_dev // depth
    side = MOS_ROWS - start_range(GRID - 1, MOS_ROWS - LANES)[0]
    reach_up, reach_down = {}, {}
    for block in range(groups):
        rows = [covered_rows(group, beams, side, block) for group in range(groups)]
        for z in range(groups):
            reach_up[z, block] = max(high for _, high in rows[: z + 1])
            reach_down[z, block] = min(low for low, _ in rows[z:])
    dma = pltpu.SemaphoreType.DMA
    any_space = pl.BlockSpec(memory_space=pl.ANY)
    return pl.pallas_call(
        functools.partial(
            exchange_kernel,
            groups=groups,
            tiles=tiles,
            depth=depth,
            reach_up=reach_up,
            reach_down=reach_down,
        ),
        in_specs=[any_space] * 3,
        out_specs=[any_space] * 3,
        out_shape=[
            jax.ShapeDtypeStruct((tiles * ch_dev, tile_rows, LANES), jnp.float32),
            jax.ShapeDtypeStruct((tiles * ch_dev, tile_rows, LANES), jnp.int32),
            jax.ShapeDtypeStruct((groups * beams, tile_rows, LANES), jnp.float32),
        ],
        scratch_shapes=[
            pltpu.VMEM((groups, ch_dev, MOS_ROWS, LANES), jnp.float32),
            pltpu.VMEM((groups - 1, ch_dev, MOS_ROWS, LANES), jnp.float32),
            pltpu.VMEM((groups - 1, ch_dev, MOS_ROWS, LANES), jnp.float32),
            pltpu.VMEM((tiles, ch_dev, tile_rows, LANES), jnp.float32),
            dma((steps,)),
            dma((3,)),
            dma((steps, groups)),
            dma((steps, groups)),
            dma((groups,)),
            dma((groups,)),
            dma((tiles - 1,)),
            dma((tiles - 1,)),
            dma((tiles - 1,)),
            dma((tiles - 1,)),
            dma((groups - 1,)),
            dma((groups - 1,)),
        ],
        compiler_params=pltpu.CompilerParams(
            collective_id=0, has_side_effects=True, vmem_limit_bytes=56 << 20
        ),
        name="exchange",
    )(sums, flags, logs)


def solve_cubic(normal_matrix, right_side):
    factor = {}
    for outer in range(4):
        for inner in range(outer + 1):
            value = normal_matrix[outer, inner]
            for other in range(inner):
                value = value - factor[outer, other] * factor[inner, other]
            if outer == inner:
                factor[outer, outer] = jnp.sqrt(value)
            else:
                factor[outer, inner] = value / factor[inner, inner]
    forward = []
    for outer in range(4):
        value = right_side[outer]
        for other in range(outer):
            value = value - factor[outer, other] * forward[other]
        forward.append(value / factor[outer, outer])
    backward = [None] * 4
    for outer in range(3, -1, -1):
        value = forward[outer]
        for other in range(outer + 1, 4):
            value = value - factor[other, outer] * backward[other]
        backward[outer] = value / factor[outer, outer]
    return backward


POLYNOMIALS = (
    {0: 1.0},
    {1: 1.0},
    {0: -0.5, 2: 1.5},
    {1: -1.5, 3: 2.5},
)


def fit_kernel(where_ref, regression_ref, sky_ref, flag_ref, log_ref, out_ref, total_ref, *, slope):
    channels, rows, _ = sky_ref.shape
    piece = 8 if rows % 8 == 0 else rows
    run = 16
    first = where_ref[0]
    beams = [(r * GRID, q) for r in range(GRID) for q in range(3)]

    def totals(index, carry):
        start = index * run
        exponent = 1.0 + slope * start.astype(jnp.float32)
        for part in range(rows // piece):
            span = pl.ds(part * piece, piece)
            total = [jnp.zeros((piece, LANES), jnp.float32)] * run
            for begin, q in beams:
                logs = log_ref[begin + q + first, span, :]
                value = jnp.exp((2.0 * exponent) * logs)
                ratio = jnp.exp((2.0 * slope) * logs)
                for k in range(run):
                    total[k] = total[k] + value
                    if k < run - 1:
                        value = value * ratio
            for k in range(run):
                total_ref[start + k, span, :] = total[k]
        return carry

    lax.fori_loop(0, channels // run, totals, 0)

    def position(channel):
        return (2.0 * channel.astype(jnp.float32) + 1.0) * (1.0 / channels) - 1.0

    def gather(channel, carry):
        powers, rights = list(carry[:7]), list(carry[7:])
        x = position(channel)
        open_sky = 1.0 - flag_ref[channel].astype(jnp.float32)
        total = total_ref[channel]
        sky = open_sky * sky_ref[channel] / total
        total_ref[channel] = sky
        chosen = regression_ref[channel].astype(jnp.float32)
        weight = total * (chosen * open_sky + 0.01)
        right = weight * sky
        for k in range(7):
            powers[k] = powers[k] + weight
            if k < 6:
                weight = weight * x
        for k in range(4):
            rights[k] = rights[k] + right
            if k < 3:
                right = right * x
        return tuple(powers) + tuple(rights)

    zero = jnp.zeros((rows, LANES), jnp.float32)
    sums = lax.fori_loop(0, channels, gather, (zero,) * 11, unroll=4)
    powers, rights = sums[:7], sums[7:]
    normal = {}
    for outer in range(4):
        for inner in range(outer + 1):
            terms = {}
            for a, u in POLYNOMIALS[outer].items():
                for b, v in POLYNOMIALS[inner].items():
                    terms[a + b] = terms.get(a + b, 0.0) + u * v
            normal[outer, inner] = sum(v * powers[k] for k, v in terms.items())
    right_side = [sum(v * rights[k] for k, v in POLYNOMIALS[o].items()) for o in range(4)]
    fitted = solve_cubic(normal, right_side)

    def residual(channel):
        x = position(channel)
        square = x * x
        continuum = (
            fitted[0]
            + x * fitted[1]
            + (0.5 * (3.0 * square - 1.0)) * fitted[2]
            + (0.5 * (5.0 * square * x - 3.0 * x)) * fitted[3]
        )
        return total_ref[channel] - continuum

    def smooth(channel, carry):
        before, here = carry
        after = residual(channel + 1)
        out_ref[channel] = 0.25 * before + 0.5 * here + 0.25 * after
        return here, after

    before, here = lax.fori_loop(
        0, channels - 1, smooth, (zero, residual(jnp.int32(0))), unroll=3
    )
    out_ref[channels - 1] = 0.25 * before + 0.5 * here


def fit(where, regression, sky, flags, logs):
    channels = sky.shape[0]
    smem = pl.BlockSpec(memory_space=pltpu.SMEM)
    vmem = pl.BlockSpec(memory_space=pltpu.VMEM)
    return pl.pallas_call(
        functools.partial(fit_kernel, slope=0.5 / (channels - 1)),
        in_specs=[smem, smem, vmem, vmem, vmem],
        out_specs=vmem,
        out_shape=jax.ShapeDtypeStruct(sky.shape, jnp.float32),
        scratch_shapes=[pltpu.VMEM(sky.shape, jnp.float32)],
        compiler_params=pltpu.CompilerParams(vmem_limit_bytes=48 << 20),
        name="fit",
    )(where, regression, sky, flags, logs)


def local(
    images, beam_weight, offsets, rejected_indicator, regression_indicator, *, groups, tiles
):
    ch_dev = images.shape[0]
    channels = regression_indicator.shape[0]
    tile_rows = MOS_ROWS // tiles
    tile = lax.axis_index("chan")
    group = lax.axis_index("beam")
    where = jnp.stack([tile * ch_dev, tile * tile_rows]).astype(jnp.int32)
    sums, logs = place(where, offsets, images, beam_weight, groups, tile_rows, channels)
    flags = rejected_indicator.reshape(ch_dev, tiles, tile_rows, rejected_indicator.shape[2])
    sky, flags, logs = exchange(sums, flags, logs, groups, tiles)
    return fit(group[None].astype(jnp.int32), regression_indicator, sky, flags, logs)


def solution(mesh):
    in_specs = (
        P("chan", "beam", None, None),
        P("beam", None, None),
        P("beam", None),
        P("chan", None, "beam"),
        P(),
    )
    out_specs = P(None, "chan", "beam")
    body = functools.partial(local, groups=mesh.shape["beam"], tiles=mesh.shape["chan"])
    return jax.shard_map(body, mesh=mesh, in_specs=in_specs, out_specs=out_specs, check_vma=False)
```

```python
import functools

import jax
import jax.numpy as jnp
from jax import lax
from jax.experimental import pallas as pl
from jax.experimental.pallas import tpu as pltpu
from jax.sharding import PartitionSpec as P

MOS_ROWS = 192
MOS_COLS = 512
GRID = 6
JITTER = 16
LANES = 128
OUTSIDE = -1.0e4
PAD = 40
SLOTS = 3
MESH = pl.DeviceIdType.MESH


def start_range(position, span):
    if position == 0:
        return 0, 0
    if position == GRID - 1:
        return span, span
    middle = position * span // (GRID - 1)
    return max(0, middle - JITTER), min(span, middle + JITTER)


def covered_rows(group, beams_each, side, block):
    first, last = MOS_ROWS, 0
    for beam in range(group * beams_each, (group + 1) * beams_each):
        low, high = start_range(beam % GRID, MOS_COLS - side)
        if high + side <= block * LANES or low >= (block + 1) * LANES:
            continue
        low, high = start_range(beam // GRID, MOS_ROWS - side)
        first, last = min(first, low), max(last, high + side)
    return first // 8 * 8, min(MOS_ROWS, -(-last // 8) * 8)


def tiles_kernel(where_ref, offsets_ref, weight_ref, tiles_ref, plane_ref):
    blocks, beams, tile_rows, _ = tiles_ref.shape
    side = weight_ref.shape[1]
    piece = 64
    lane = lax.broadcasted_iota(jnp.int32, (piece, LANES), 1)

    def spread(beam, carry):
        row, col = offsets_ref[beam, 0], offsets_ref[beam, 1]
        block, shift = lax.shift_right_logical(col, 7), jnp.bitwise_and(col, LANES - 1)
        plane_ref[...] = jnp.full(plane_ref.shape, OUTSIDE, jnp.float32)

        def part(index, inner):
            start = pl.multiple_of(index * piece, piece)
            value = jnp.log(weight_ref[beam, pl.ds(start, piece), :])
            value = pltpu.roll(value, shift, 1)
            plane_ref[block, pl.ds(row + start, piece), :] = jnp.where(
                lane >= shift, value, OUTSIDE
            )

            @pl.when(block < blocks - 1)
            def _():
                plane_ref[block + 1, pl.ds(row + start, piece), :] = jnp.where(
                    lane < shift, value, OUTSIDE
                )

            return inner

        lax.fori_loop(0, side // piece, part, 0)
        tiles_ref[:, beam, :, :] = plane_ref[:, pl.ds(where_ref[0], tile_rows), :]
        return carry

    lax.fori_loop(0, beams, spread, 0)


def log_tiles(where, offsets, beam_weight, blocks, tile_rows):
    beams = beam_weight.shape[0]
    smem = pl.BlockSpec(memory_space=pltpu.SMEM)
    vmem = pl.BlockSpec(memory_space=pltpu.VMEM)
    return pl.pallas_call(
        tiles_kernel,
        in_specs=[smem, smem, vmem],
        out_specs=vmem,
        out_shape=jax.ShapeDtypeStruct((blocks, beams, tile_rows, LANES), jnp.float32),
        scratch_shapes=[pltpu.VMEM((blocks, MOS_ROWS, LANES), jnp.float32)],
        name="log_tiles",
    )(where, offsets, beam_weight)


def exchange_kernel(
    offsets_ref,
    weight_ref,
    image_ref,
    flags_ref,
    logs_ref,
    sky_out,
    flag_out,
    total_out,
    own,
    up,
    down,
    rowed,
    fetched,
    own_logs,
    padded,
    arrived,
    total,
    own_sem,
    keep_sem,
    up_recv,
    down_recv,
    up_send,
    down_send,
    sky_send,
    sky_recv,
    flag_send,
    flag_recv,
    log_send,
    log_recv,
    *,
    groups,
    tiles,
    depth,
    reach_up,
    reach_down,
    slope,
):
    group = lax.axis_index("beam")
    tile = lax.axis_index("chan")
    ch_dev = image_ref.shape[0]
    side = weight_ref.shape[1]
    tile_rows = flags_ref.shape[2]
    beams = logs_ref.shape[1]
    steps = ch_dev // depth
    run = tiles * depth

    others = [lax.rem(tile + k, tiles) for k in range(1, tiles)]
    columns = [lax.rem(group + k, groups) for k in range(1, groups)]

    barrier = pltpu.get_barrier_semaphore()
    for other in others:
        pl.semaphore_signal(barrier, inc=1, device_id={"chan": other}, device_id_type=MESH)
    for other in columns:
        pl.semaphore_signal(barrier, inc=1, device_id={"beam": other}, device_id_type=MESH)

    def load(step):
        slot = lax.rem(step, SLOTS)
        return pltpu.make_async_copy(
            image_ref.at[pl.ds(step * depth, depth)], fetched.at[slot], own_sem.at[slot]
        )

    for step in range(min(SLOTS, steps)):
        load(step).start()
    mine = pl.ds(tile * ch_dev, ch_dev)
    kept = [
        pltpu.make_async_copy(flags_ref.at[:, tile], flag_out.at[mine], keep_sem.at[0]),
        pltpu.make_async_copy(
            logs_ref.at[group], arrived.at[pl.ds(group * beams, beams)], keep_sem.at[1]
        ),
    ]
    for copy in kept:
        copy.start()
    pl.semaphore_wait(barrier, len(others) + len(columns))

    small = []
    for k, other in enumerate(columns):
        small.append(
            pltpu.make_async_remote_copy(
                src_ref=logs_ref.at[other],
                dst_ref=arrived.at[pl.ds(group * beams, beams)],
                send_sem=log_send.at[k],
                recv_sem=log_recv.at[k],
                device_id={"beam": other},
                device_id_type=MESH,
            )
        )
    for k, other in enumerate(others):
        small.append(
            pltpu.make_async_remote_copy(
                src_ref=flags_ref.at[:, other],
                dst_ref=flag_out.at[mine],
                send_sem=flag_send.at[k],
                recv_sem=flag_recv.at[k],
                device_id={"chan": other},
                device_id_type=MESH,
            )
        )
    for copy in small:
        copy.start()

    own_logs[...] = jnp.log(weight_ref[...])
    padded[...] = jnp.zeros(padded.shape, jnp.float32)
    lane = lax.broadcasted_iota(jnp.int32, (1, LANES), 1)

    def place(z, step):
        load(step).wait()
        slot = lax.rem(step, SLOTS)
        exponent = 1.0 + slope * (tile * ch_dev + step * depth).astype(jnp.float32)

        def weigh(beam, carry):
            logs = own_logs[beam]
            response = jnp.exp(exponent * logs)
            ratio = jnp.exp(slope * logs)
            for channel in range(depth):
                padded[channel, beam, PAD : PAD + side, :] = (
                    fetched[slot, channel, beam] * response
                )
                response = response * ratio
            return carry

        lax.fori_loop(0, beams, weigh, 0)

        @pl.when(step + SLOTS < steps)
        def _():
            load(step + SLOTS).start()

        span = pl.ds(step * depth, depth)
        own[:, span] = jnp.zeros((groups, depth, MOS_ROWS, LANES), jnp.float32)
        for beam in range(beams):
            place_row, place_col = divmod(z * beams + beam, GRID)
            low, high = start_range(place_row, MOS_ROWS - side)
            first, last = low // 8 * 8, -(-(high + side) // 8) * 8
            row = jnp.clip(offsets_ref[beam, 0], low, high)
            low, high = start_range(place_col, MOS_COLS - side)
            block = low // LANES
            values = [
                padded[channel, beam, pl.ds(PAD + first - row, last - first), :]
                for channel in range(depth)
            ]
            if low == high and low % LANES == 0:
                for channel, value in enumerate(values):
                    own[block, step * depth + channel, first:last, :] += value
                continue
            shift = jnp.clip(offsets_ref[beam, 1], low, high) - block * LANES
            values = [pltpu.roll(value, shift, 1) for value in values]
            for target, inside in ((block, lane >= shift), (block + 1, lane < shift)):
                for channel, value in enumerate(values):
                    own[target, step * depth + channel, first:last, :] += jnp.where(
                        inside, value, 0.0
                    )

    def add_weights(z, step):
        start = step * run
        exponent = 1.0 + slope * start.astype(jnp.float32)
        piece = 8 if tile_rows % 8 == 0 else tile_rows
        for part in range(tile_rows // piece):
            rows = pl.ds(part * piece, piece)
            sums = [jnp.zeros((piece, LANES), jnp.float32)] * run
            for place_row in range(GRID):
                for place_col in range(z, z + 3):
                    logs = arrived[place_row * GRID + place_col, rows, :]
                    value = jnp.exp((2.0 * exponent) * logs)
                    ratio = jnp.exp((2.0 * slope) * logs)
                    for k in range(run):
                        sums[k] = sums[k] + value
                        if k < run - 1:
                            value = value * ratio
            for k in range(run):
                total[start + k, rows, :] = sums[k]

    def up_copy(z, block, step):
        span, rows = pl.ds(step * depth, depth), pl.ds(0, reach_up[z, block])
        source = own.at[block, span, rows] if z == 0 else up.at[block - 1, span, rows]
        return pltpu.make_async_remote_copy(
            src_ref=source,
            dst_ref=up.at[block - 1, span, rows],
            send_sem=up_send.at[block],
            recv_sem=up_recv.at[step, block],
            device_id={"beam": z + 1},
            device_id_type=MESH,
        )

    def down_copy(z, block, step):
        first = reach_down[z, block]
        span, rows = pl.ds(step * depth, depth), pl.ds(first, MOS_ROWS - first)
        source = own.at[block, span, rows] if z == groups - 1 else down.at[block, span, rows]
        return pltpu.make_async_remote_copy(
            src_ref=source,
            dst_ref=down.at[block, span, rows],
            send_sem=down_send.at[block],
            recv_sem=down_recv.at[step, block],
            device_id={"beam": z - 1},
            device_id_type=MESH,
        )

    def sky_copy(k, other, span):
        return pltpu.make_async_remote_copy(
            src_ref=rowed.at[other, span],
            dst_ref=sky_out.at[pl.ds(tile * ch_dev + span.start, span.size)],
            send_sem=sky_send.at[k],
            recv_sem=sky_recv.at[k],
            device_id={"chan": other},
            device_id_type=MESH,
        )

    for z in range(groups):

        @pl.when(group == z)
        def _(z=z):
            lower = 2 * z < groups
            up_lag, down_lag = (0, 2) if lower else (2, 0)
            last_lag = 6 if z in (0, groups - 1) else 3

            def pass_up(step):
                span = pl.ds(step * depth, depth)
                for block in range(groups - 1, z, -1):
                    if z > 0:
                        old, new = reach_up[z - 1, block], reach_up[z, block]
                        up_copy(z - 1, block, step).wait_recv()
                        up[block - 1, span, 0:old, :] += own[block, span, 0:old, :]
                        if new > old:
                            up[block - 1, span, old:new, :] = own[block, span, old:new, :]
                    up_copy(z, block, step).start()

            def pass_down(step):
                span = pl.ds(step * depth, depth)
                for block in range(z):
                    if z < groups - 1:
                        old, new = reach_down[z + 1, block], reach_down[z, block]
                        down_copy(z + 1, block, step).wait_recv()
                        down[block, span, old:, :] += own[block, span, old:, :]
                        if new < old:
                            down[block, span, new:old, :] = own[block, span, new:old, :]
                    down_copy(z, block, step).start()

            def finish(step):
                span = pl.ds(step * depth, depth)
                if z > 0:
                    old = reach_up[z - 1, z]
                    up_copy(z - 1, z, step).wait_recv()
                    own[z, span, 0:old, :] += up[z - 1, span, 0:old, :]
                if z < groups - 1:
                    old = reach_down[z + 1, z]
                    down_copy(z + 1, z, step).wait_recv()
                    own[z, span, old:, :] += down[z, span, old:, :]
                for index in range(tiles):
                    rowed[index, span, :, :] = own[
                        z, span, index * tile_rows : (index + 1) * tile_rows, :
                    ]
                for k, other in enumerate(others):
                    sky_copy(k, other, span).start()

            def work(turn, carry):
                @pl.when(turn < steps)
                def _():
                    place(z, turn)

                for lag, act in ((up_lag, pass_up), (down_lag, pass_down), (last_lag, finish)):

                    @pl.when(jnp.logical_and(turn >= lag, turn < steps + lag))
                    def _(lag=lag, act=act):
                        act(turn - lag)

                @pl.when(turn == 1)
                def _():
                    for copy in small[: groups - 1]:
                        copy.wait()
                    kept[1].wait()

                @pl.when(jnp.logical_and(turn >= 1, turn < steps + 1))
                def _():
                    add_weights(z, turn - 1)

                return carry

            lax.fori_loop(0, steps + last_lag, work, 0)
            for block in range(z + 1, groups):
                ref = up.at[block - 1, :, pl.ds(0, reach_up[z, block])]
                pltpu.make_async_copy(ref, ref, up_send.at[block]).wait()
            for block in range(z):
                first = reach_down[z, block]
                ref = down.at[block, :, pl.ds(first, MOS_ROWS - first)]
                pltpu.make_async_copy(ref, ref, down_send.at[block]).wait()

    last = [
        pltpu.make_async_copy(rowed.at[tile], sky_out.at[mine], keep_sem.at[2]),
        pltpu.make_async_copy(total, total_out, keep_sem.at[3]),
        kept[0],
    ]
    for copy in last[:2]:
        copy.start()
    for copy in small[groups - 1 :]:
        copy.wait()
    for k, other in enumerate(others):
        sky_copy(k, other, pl.ds(0, ch_dev)).wait()
    for copy in last:
        copy.wait()


def exchange(offsets, beam_weight, images, flags, logs, groups, tiles):
    ch_dev, _, side, _ = images.shape
    tile_rows = flags.shape[2]
    beams = logs.shape[1]
    depth = 2
    steps = ch_dev // depth
    reach_up, reach_down = {}, {}
    for block in range(groups):
        rows = [covered_rows(group, beams, side, block) for group in range(groups)]
        for z in range(groups):
            reach_up[z, block] = max(high for _, high in rows[: z + 1])
            reach_down[z, block] = min(low for low, _ in rows[z:])
    dma = pltpu.SemaphoreType.DMA
    any_space = pl.BlockSpec(memory_space=pl.ANY)
    return pl.pallas_call(
        functools.partial(
            exchange_kernel,
            groups=groups,
            tiles=tiles,
            depth=depth,
            reach_up=reach_up,
            reach_down=reach_down,
            slope=0.5 / (tiles * ch_dev - 1),
        ),
        in_specs=[
            pl.BlockSpec(memory_space=pltpu.SMEM),
            pl.BlockSpec(memory_space=pltpu.VMEM),
            any_space,
            any_space,
            any_space,
        ],
        out_specs=[any_space] * 3,
        out_shape=[
            jax.ShapeDtypeStruct((tiles * ch_dev, tile_rows, LANES), jnp.float32),
            jax.ShapeDtypeStruct((tiles * ch_dev, tile_rows, LANES), jnp.int32),
            jax.ShapeDtypeStruct((tiles * ch_dev, tile_rows, LANES), jnp.float32),
        ],
        scratch_shapes=[
            pltpu.VMEM((groups, ch_dev, MOS_ROWS, LANES), jnp.float32),
            pltpu.VMEM((groups - 1, ch_dev, MOS_ROWS, LANES), jnp.float32),
            pltpu.VMEM((groups - 1, ch_dev, MOS_ROWS, LANES), jnp.float32),
            pltpu.VMEM((tiles, ch_dev, tile_rows, LANES), jnp.float32),
            pltpu.VMEM((SLOTS, depth, beams, side, side), jnp.float32),
            pltpu.VMEM((beams, side, side), jnp.float32),
            pltpu.VMEM((depth, beams, PAD + side + PAD, side), jnp.float32),
            pltpu.VMEM((groups * beams, tile_rows, LANES), jnp.float32),
            pltpu.VMEM((tiles * ch_dev, tile_rows, LANES), jnp.float32),
            dma((SLOTS,)),
            dma((4,)),
            dma((steps, groups)),
            dma((steps, groups)),
            dma((groups,)),
            dma((groups,)),
            dma((tiles - 1,)),
            dma((tiles - 1,)),
            dma((tiles - 1,)),
            dma((tiles - 1,)),
            dma((groups - 1,)),
            dma((groups - 1,)),
        ],
        compiler_params=pltpu.CompilerParams(
            collective_id=0, has_side_effects=True, vmem_limit_bytes=56 << 20
        ),
        name="exchange",
    )(offsets, beam_weight, images, flags, logs)


def solve_cubic(normal_matrix, right_side):
    factor = {}
    for outer in range(4):
        for inner in range(outer + 1):
            value = normal_matrix[outer, inner]
            for other in range(inner):
                value = value - factor[outer, other] * factor[inner, other]
            if outer == inner:
                factor[outer, outer] = jnp.sqrt(value)
            else:
                factor[outer, inner] = value / factor[inner, inner]
    forward = []
    for outer in range(4):
        value = right_side[outer]
        for other in range(outer):
            value = value - factor[outer, other] * forward[other]
        forward.append(value / factor[outer, outer])
    backward = [None] * 4
    for outer in range(3, -1, -1):
        value = forward[outer]
        for other in range(outer + 1, 4):
            value = value - factor[other, outer] * backward[other]
        backward[outer] = value / factor[outer, outer]
    return backward


POLYNOMIALS = (
    {0: 1.0},
    {1: 1.0},
    {0: -0.5, 2: 1.5},
    {1: -1.5, 3: 2.5},
)


def fit_kernel(regression_ref, sky_ref, flag_ref, weights_ref, out_ref, total_ref):
    channels, rows, _ = sky_ref.shape

    def position(channel):
        return (2.0 * channel.astype(jnp.float32) + 1.0) * (1.0 / channels) - 1.0

    def gather(channel, carry):
        powers, rights = list(carry[:7]), list(carry[7:])
        x = position(channel)
        open_sky = 1.0 - flag_ref[channel].astype(jnp.float32)
        total = weights_ref[channel]
        sky = open_sky * sky_ref[channel] / total
        total_ref[channel] = sky
        chosen = regression_ref[channel].astype(jnp.float32)
        weight = total * (chosen * open_sky + 0.01)
        right = weight * sky
        for k in range(7):
            powers[k] = powers[k] + weight
            if k < 6:
                weight = weight * x
        for k in range(4):
            rights[k] = rights[k] + right
            if k < 3:
                right = right * x
        return tuple(powers) + tuple(rights)

    zero = jnp.zeros((rows, LANES), jnp.float32)
    sums = lax.fori_loop(0, channels, gather, (zero,) * 11, unroll=4)
    powers, rights = sums[:7], sums[7:]
    normal = {}
    for outer in range(4):
        for inner in range(outer + 1):
            terms = {}
            for a, u in POLYNOMIALS[outer].items():
                for b, v in POLYNOMIALS[inner].items():
                    terms[a + b] = terms.get(a + b, 0.0) + u * v
            normal[outer, inner] = sum(v * powers[k] for k, v in terms.items())
    right_side = [sum(v * rights[k] for k, v in POLYNOMIALS[o].items()) for o in range(4)]
    fitted = solve_cubic(normal, right_side)

    def residual(channel):
        x = position(channel)
        square = x * x
        continuum = (
            fitted[0]
            + x * fitted[1]
            + (0.5 * (3.0 * square - 1.0)) * fitted[2]
            + (0.5 * (5.0 * square * x - 3.0 * x)) * fitted[3]
        )
        return total_ref[channel] - continuum

    def smooth(channel, carry):
        before, here = carry
        after = residual(channel + 1)
        out_ref[channel] = 0.25 * before + 0.5 * here + 0.25 * after
        return here, after

    before, here = lax.fori_loop(
        0, channels - 1, smooth, (zero, residual(jnp.int32(0))), unroll=3
    )
    out_ref[channels - 1] = 0.25 * before + 0.5 * here


def fit(regression, sky, flags, total):
    smem = pl.BlockSpec(memory_space=pltpu.SMEM)
    vmem = pl.BlockSpec(memory_space=pltpu.VMEM)
    return pl.pallas_call(
        fit_kernel,
        in_specs=[smem, vmem, vmem, vmem],
        out_specs=vmem,
        out_shape=jax.ShapeDtypeStruct(sky.shape, jnp.float32),
        scratch_shapes=[pltpu.VMEM(sky.shape, jnp.float32)],
        compiler_params=pltpu.CompilerParams(vmem_limit_bytes=48 << 20),
        name="fit",
    )(regression, sky, flags, total)


def local(
    images, beam_weight, offsets, rejected_indicator, regression_indicator, *, groups, tiles
):
    ch_dev = images.shape[0]
    tile_rows = MOS_ROWS // tiles
    where = (lax.axis_index("chan") * tile_rows).astype(jnp.int32)[None]
    logs = log_tiles(where, offsets, beam_weight, groups, tile_rows)
    flags = rejected_indicator.reshape(ch_dev, tiles, tile_rows, rejected_indicator.shape[2])
    sky, flags, total = exchange(offsets, beam_weight, images, flags, logs, groups, tiles)
    return fit(regression_indicator, sky, flags, total)


def solution(mesh):
    in_specs = (
        P("chan", "beam", None, None),
        P("beam", None, None),
        P("beam", None),
        P("chan", None, "beam"),
        P(),
    )
    out_specs = P(None, "chan", "beam")
    body = functools.partial(local, groups=mesh.shape["beam"], tiles=mesh.shape["chan"])
    return jax.shard_map(body, mesh=mesh, in_specs=in_specs, out_specs=out_specs, check_vma=False)
```

```python
import functools

import jax
import jax.numpy as jnp
from jax import lax
from jax.experimental import pallas as pl
from jax.experimental.pallas import tpu as pltpu
from jax.sharding import PartitionSpec as P

MOS_ROWS = 192
MOS_COLS = 512
GRID = 6
JITTER = 16
LANES = 128
OUTSIDE = -1.0e4
PAD = 40
SLOTS = 3
MESH = pl.DeviceIdType.MESH


def start_range(position, span):
    if position == 0:
        return 0, 0
    if position == GRID - 1:
        return span, span
    middle = position * span // (GRID - 1)
    return max(0, middle - JITTER), min(span, middle + JITTER)


def covered_rows(group, beams_each, side, block):
    first, last = MOS_ROWS, 0
    for beam in range(group * beams_each, (group + 1) * beams_each):
        low, high = start_range(beam % GRID, MOS_COLS - side)
        if high + side <= block * LANES or low >= (block + 1) * LANES:
            continue
        low, high = start_range(beam // GRID, MOS_ROWS - side)
        first, last = min(first, low), max(last, high + side)
    return first // 8 * 8, min(MOS_ROWS, -(-last // 8) * 8)


def reaching(group, beams_each, side, block):
    found = []
    for place in range(beams_each):
        low, high = start_range((group * beams_each + place) % GRID, MOS_COLS - side)
        if high + side > block * LANES and low < (block + 1) * LANES:
            found.append(place)
    return found


def foldable(group, beams_each, side, block, upward):
    if block == group:
        return False
    for place in reaching(group, beams_each, side, block):
        beam = group * beams_each + place
        low, high = start_range(beam // GRID, MOS_ROWS - side)
        left, right = start_range(beam % GRID, MOS_COLS - side)
        if upward and high > 0 and right + side - block * LANES > LANES // 2:
            return False
        if not upward and low < MOS_ROWS - side and left - block * LANES < LANES // 2:
            return False
    return True


def tiles_kernel(where_ref, offsets_ref, weight_ref, tiles_ref, plane_ref):
    blocks, beams, tile_rows, _ = tiles_ref.shape
    side = weight_ref.shape[1]
    piece = 64
    lane = lax.broadcasted_iota(jnp.int32, (piece, LANES), 1)

    def spread(beam, carry):
        row, col = offsets_ref[beam, 0], offsets_ref[beam, 1]
        block, shift = lax.shift_right_logical(col, 7), jnp.bitwise_and(col, LANES - 1)
        plane_ref[...] = jnp.full(plane_ref.shape, OUTSIDE, jnp.float32)

        def part(index, inner):
            start = pl.multiple_of(index * piece, piece)
            value = jnp.log(weight_ref[beam, pl.ds(start, piece), :])
            value = pltpu.roll(value, shift, 1)
            plane_ref[block, pl.ds(row + start, piece), :] = jnp.where(
                lane >= shift, value, OUTSIDE
            )

            @pl.when(block < blocks - 1)
            def _():
                plane_ref[block + 1, pl.ds(row + start, piece), :] = jnp.where(
                    lane < shift, value, OUTSIDE
                )

            return inner

        lax.fori_loop(0, side // piece, part, 0)
        tiles_ref[:, beam, :, :] = plane_ref[:, pl.ds(where_ref[0], tile_rows), :]
        return carry

    lax.fori_loop(0, beams, spread, 0)


def log_tiles(where, offsets, beam_weight, blocks, tile_rows):
    beams = beam_weight.shape[0]
    smem = pl.BlockSpec(memory_space=pltpu.SMEM)
    vmem = pl.BlockSpec(memory_space=pltpu.VMEM)
    return pl.pallas_call(
        tiles_kernel,
        in_specs=[smem, smem, vmem],
        out_specs=vmem,
        out_shape=jax.ShapeDtypeStruct((blocks, beams, tile_rows, LANES), jnp.float32),
        scratch_shapes=[pltpu.VMEM((blocks, MOS_ROWS, LANES), jnp.float32)],
        name="log_tiles",
    )(where, offsets, beam_weight)


def exchange_kernel(
    offsets_ref,
    weight_ref,
    image_ref,
    flags_ref,
    logs_ref,
    sky_out,
    flag_out,
    total_out,
    own,
    up,
    down,
    rowed,
    fetched,
    own_logs,
    padded,
    arrived,
    total,
    own_sem,
    keep_sem,
    up_recv,
    down_recv,
    up_send,
    down_send,
    sky_send,
    sky_recv,
    flag_send,
    flag_recv,
    log_send,
    log_recv,
    *,
    groups,
    tiles,
    depth,
    reach_up,
    reach_down,
    fold_up,
    fold_down,
    slope,
):
    group = lax.axis_index("beam")
    tile = lax.axis_index("chan")
    ch_dev = image_ref.shape[0]
    side = weight_ref.shape[1]
    tile_rows = flags_ref.shape[2]
    beams = logs_ref.shape[1]
    steps = ch_dev // depth
    run = tiles * depth

    others = [lax.rem(tile + k, tiles) for k in range(1, tiles)]
    columns = [lax.rem(group + k, groups) for k in range(1, groups)]

    barrier = pltpu.get_barrier_semaphore()
    for other in others:
        pl.semaphore_signal(barrier, inc=1, device_id={"chan": other}, device_id_type=MESH)
    for other in columns:
        pl.semaphore_signal(barrier, inc=1, device_id={"beam": other}, device_id_type=MESH)

    def load(step):
        slot = lax.rem(step, SLOTS)
        return pltpu.make_async_copy(
            image_ref.at[pl.ds(step * depth, depth)], fetched.at[slot], own_sem.at[slot]
        )

    for step in range(min(SLOTS, steps)):
        load(step).start()
    mine = pl.ds(tile * ch_dev, ch_dev)
    kept = [
        pltpu.make_async_copy(flags_ref.at[:, tile], flag_out.at[mine], keep_sem.at[0]),
        pltpu.make_async_copy(
            logs_ref.at[group], arrived.at[pl.ds(group * beams, beams)], keep_sem.at[1]
        ),
    ]
    for copy in kept:
        copy.start()
    pl.semaphore_wait(barrier, len(others) + len(columns))

    def log_copy(source, k, beam):
        return pltpu.make_async_remote_copy(
            src_ref=logs_ref.at[(source + k) % groups, beam],
            dst_ref=arrived.at[source * beams + beam],
            send_sem=log_send.at[k - 1],
            recv_sem=log_recv.at[k - 1],
            device_id={"beam": (source + k) % groups},
            device_id_type=MESH,
        )

    small = []
    for k, other in enumerate(others):
        small.append(
            pltpu.make_async_remote_copy(
                src_ref=flags_ref.at[:, other],
                dst_ref=flag_out.at[mine],
                send_sem=flag_send.at[k],
                recv_sem=flag_recv.at[k],
                device_id={"chan": other},
                device_id_type=MESH,
            )
        )
    for copy in small:
        copy.start()

    own_logs[...] = jnp.log(weight_ref[...])
    padded[...] = jnp.zeros(padded.shape, jnp.float32)
    lane = lax.broadcasted_iota(jnp.int32, (1, LANES), 1)

    def place(z, step):
        load(step).wait()
        slot = lax.rem(step, SLOTS)
        exponent = 1.0 + slope * (tile * ch_dev + step * depth).astype(jnp.float32)

        def weigh(beam, carry):
            logs = own_logs[beam]
            response = jnp.exp(exponent * logs)
            ratio = jnp.exp(slope * logs)
            for channel in range(depth):
                padded[channel, beam, PAD : PAD + side, :] = (
                    fetched[slot, channel, beam] * response
                )
                response = response * ratio
            return carry

        lax.fori_loop(0, beams, weigh, 0)

        @pl.when(step + SLOTS < steps)
        def _():
            load(step + SLOTS).start()

        span = pl.ds(step * depth, depth)
        own[:, span] = jnp.zeros((groups, depth, MOS_ROWS, LANES), jnp.float32)
        for beam in range(beams):
            place_row, place_col = divmod(z * beams + beam, GRID)
            low, high = start_range(place_row, MOS_ROWS - side)
            first, last = low // 8 * 8, -(-(high + side) // 8) * 8
            row = jnp.clip(offsets_ref[beam, 0], low, high)
            low, high = start_range(place_col, MOS_COLS - side)
            block = low // LANES
            values = [
                padded[channel, beam, pl.ds(PAD + first - row, last - first), :]
                for channel in range(depth)
            ]
            if low == high and low % LANES == 0:
                for channel, value in enumerate(values):
                    own[block, step * depth + channel, first:last, :] += value
                continue
            shift = jnp.clip(offsets_ref[beam, 1], low, high) - block * LANES
            values = [pltpu.roll(value, shift, 1) for value in values]
            for target, inside in ((block, lane >= shift), (block + 1, lane < shift)):
                for channel, value in enumerate(values):
                    own[target, step * depth + channel, first:last, :] += jnp.where(
                        inside, value, 0.0
                    )

    def add_weights(z, step):
        start = step * run
        exponent = 1.0 + slope * start.astype(jnp.float32)
        piece = 8 if tile_rows % 8 == 0 else tile_rows
        for part in range(tile_rows // piece):
            rows = pl.ds(part * piece, piece)
            sums = [jnp.zeros((piece, LANES), jnp.float32)] * run
            for source in range(groups):
                for beam in reaching(source, beams, side, z):
                    logs = arrived[source * beams + beam, rows, :]
                    value = jnp.exp((2.0 * exponent) * logs)
                    ratio = jnp.exp((2.0 * slope) * logs)
                    for k in range(run):
                        sums[k] = sums[k] + value
                        if k < run - 1:
                            value = value * ratio
            for k in range(run):
                total[start + k, rows, :] = sums[k]

    def unfold_up(z, block, span):
        last = reach_up[z - 1, block]
        if z != 1 or block not in fold_up:
            return last
        half = last - side
        both = up[block - 1, span, side:last, :]
        up[block - 1, span, side:last, :] = jnp.where(lane < LANES // 2, both, 0.0)
        up[block - 1, span, last : last + half, :] = pltpu.roll(
            jnp.where(lane < LANES // 2, 0.0, both), LANES // 2, 2
        )
        return last + half

    def unfold_down(z, block, span):
        first, edge = reach_down[z + 1, block], MOS_ROWS - side
        if z != groups - 2 or block not in fold_down:
            return first
        both = down[block, span, first:edge, :]
        down[block, span, first:edge, :] = jnp.where(lane < LANES // 2, 0.0, both)
        down[block, span, 2 * first - edge : first, :] = pltpu.roll(
            jnp.where(lane < LANES // 2, both, 0.0), LANES // 2, 2
        )
        return 2 * first - edge

    def up_copy(z, block, step):
        span, rows = pl.ds(step * depth, depth), pl.ds(0, reach_up[z, block])
        source = own.at[block, span, rows] if z == 0 else up.at[block - 1, span, rows]
        return pltpu.make_async_remote_copy(
            src_ref=source,
            dst_ref=up.at[block - 1, span, rows],
            send_sem=up_send.at[block],
            recv_sem=up_recv.at[step, block],
            device_id={"beam": z + 1},
            device_id_type=MESH,
        )

    def down_copy(z, block, step):
        first = reach_down[z, block]
        span, rows = pl.ds(step * depth, depth), pl.ds(first, MOS_ROWS - first)
        source = own.at[block, span, rows] if z == groups - 1 else down.at[block, span, rows]
        return pltpu.make_async_remote_copy(
            src_ref=source,
            dst_ref=down.at[block, span, rows],
            send_sem=down_send.at[block],
            recv_sem=down_recv.at[step, block],
            device_id={"beam": z - 1},
            device_id_type=MESH,
        )

    def sky_copy(k, other, span):
        return pltpu.make_async_remote_copy(
            src_ref=rowed.at[other, span],
            dst_ref=sky_out.at[pl.ds(tile * ch_dev + span.start, span.size)],
            send_sem=sky_send.at[k],
            recv_sem=sky_recv.at[k],
            device_id={"chan": other},
            device_id_type=MESH,
        )

    for z in range(groups):

        @pl.when(group == z)
        def _(z=z):
            for k in range(1, groups):
                for beam in reaching(z, beams, side, (z + k) % groups):
                    log_copy(z, k, beam).start()
            lower = 2 * z < groups
            up_lag, down_lag = (0, 2) if lower else (2, 0)
            last_lag = 6 if z in (0, groups - 1) else 3

            def pass_up(step):
                span = pl.ds(step * depth, depth)
                for block in range(groups - 1, z, -1):
                    if z > 0:
                        up_copy(z - 1, block, step).wait_recv()
                        old, new = unfold_up(z, block, span), reach_up[z, block]
                        up[block - 1, span, 0:old, :] += own[block, span, 0:old, :]
                        if new > old:
                            up[block - 1, span, old:new, :] = own[block, span, old:new, :]
                    elif block in fold_up:
                        last = reach_up[z, block]
                        own[block, span, side:last, :] += pltpu.roll(
                            own[block, span, last : 2 * last - side, :], LANES // 2, 2
                        )
                    up_copy(z, block, step).start()

            def pass_down(step):
                span = pl.ds(step * depth, depth)
                for block in range(z):
                    if z < groups - 1:
                        down_copy(z + 1, block, step).wait_recv()
                        old, new = unfold_down(z, block, span), reach_down[z, block]
                        down[block, span, old:, :] += own[block, span, old:, :]
                        if new < old:
                            down[block, span, new:old, :] = own[block, span, new:old, :]
                    elif block in fold_down:
                        first, edge = reach_down[z, block], MOS_ROWS - side
                        own[block, span, first:edge, :] += pltpu.roll(
                            own[block, span, 2 * first - edge : first, :], LANES // 2, 2
                        )
                    down_copy(z, block, step).start()

            def finish(step):
                span = pl.ds(step * depth, depth)
                if z > 0:
                    up_copy(z - 1, z, step).wait_recv()
                    old = unfold_up(z, z, span)
                    own[z, span, 0:old, :] += up[z - 1, span, 0:old, :]
                if z < groups - 1:
                    down_copy(z + 1, z, step).wait_recv()
                    old = unfold_down(z, z, span)
                    own[z, span, old:, :] += down[z, span, old:, :]
                for index in range(tiles):
                    rowed[index, span, :, :] = own[
                        z, span, index * tile_rows : (index + 1) * tile_rows, :
                    ]
                for k, other in enumerate(others):
                    sky_copy(k, other, span).start()

            def work(turn, carry):
                @pl.when(turn < steps)
                def _():
                    place(z, turn)

                for lag, act in ((up_lag, pass_up), (down_lag, pass_down), (last_lag, finish)):

                    @pl.when(jnp.logical_and(turn >= lag, turn < steps + lag))
                    def _(lag=lag, act=act):
                        act(turn - lag)

                @pl.when(turn == 1)
                def _():
                    kept[1].wait()
                    for k in range(1, groups):
                        count = len(reaching(z, beams, side, (z + k) % groups))
                        ref = arrived.at[pl.ds(0, count)]
                        if count:
                            pltpu.make_async_copy(ref, ref, log_send.at[k - 1]).wait()
                        count = len(reaching((z - k) % groups, beams, side, z))
                        ref = arrived.at[pl.ds(0, count)]
                        if count:
                            pltpu.make_async_copy(ref, ref, log_recv.at[k - 1]).wait()

                @pl.when(jnp.logical_and(turn >= 1, turn < steps + 1))
                def _():
                    add_weights(z, turn - 1)

                return carry

            lax.fori_loop(0, steps + last_lag, work, 0)
            for block in range(z + 1, groups):
                ref = up.at[block - 1, :, pl.ds(0, reach_up[z, block])]
                pltpu.make_async_copy(ref, ref, up_send.at[block]).wait()
            for block in range(z):
                first = reach_down[z, block]
                ref = down.at[block, :, pl.ds(first, MOS_ROWS - first)]
                pltpu.make_async_copy(ref, ref, down_send.at[block]).wait()

    last = [
        pltpu.make_async_copy(rowed.at[tile], sky_out.at[mine], keep_sem.at[2]),
        pltpu.make_async_copy(total, total_out, keep_sem.at[3]),
        kept[0],
    ]
    for copy in last[:2]:
        copy.start()
    for copy in small:
        copy.wait()
    for k, other in enumerate(others):
        sky_copy(k, other, pl.ds(0, ch_dev)).wait()
    for copy in last:
        copy.wait()


def exchange(offsets, beam_weight, images, flags, logs, groups, tiles):
    ch_dev, _, side, _ = images.shape
    tile_rows = flags.shape[2]
    beams = logs.shape[1]
    depth = 2
    steps = ch_dev // depth
    reach_up, reach_down = {}, {}
    for block in range(groups):
        rows = [covered_rows(group, beams, side, block) for group in range(groups)]
        for z in range(groups):
            reach_up[z, block] = max(high for _, high in rows[: z + 1])
            reach_down[z, block] = min(low for low, _ in rows[z:])
    fold_up, fold_down = [], []
    edge = MOS_ROWS - side
    for block in range(groups):
        extra = reach_up[0, block] - side
        if extra > 0 and extra % 16 == 0 and foldable(0, beams, side, block, True):
            fold_up.append(block)
            reach_up[0, block] = side + extra // 2
        extra = edge - reach_down[groups - 1, block]
        if extra > 0 and extra % 16 == 0 and foldable(groups - 1, beams, side, block, False):
            fold_down.append(block)
            reach_down[groups - 1, block] = edge - extra // 2
    dma = pltpu.SemaphoreType.DMA
    any_space = pl.BlockSpec(memory_space=pl.ANY)
    return pl.pallas_call(
        functools.partial(
            exchange_kernel,
            groups=groups,
            tiles=tiles,
            depth=depth,
            reach_up=reach_up,
            reach_down=reach_down,
            fold_up=fold_up,
            fold_down=fold_down,
            slope=0.5 / (tiles * ch_dev - 1),
        ),
        in_specs=[
            pl.BlockSpec(memory_space=pltpu.SMEM),
            pl.BlockSpec(memory_space=pltpu.VMEM),
            any_space,
            any_space,
            any_space,
        ],
        out_specs=[any_space] * 3,
        out_shape=[
            jax.ShapeDtypeStruct((tiles * ch_dev, tile_rows, LANES), jnp.float32),
            jax.ShapeDtypeStruct((tiles * ch_dev, tile_rows, LANES), jnp.int32),
            jax.ShapeDtypeStruct((tiles * ch_dev, tile_rows, LANES), jnp.float32),
        ],
        scratch_shapes=[
            pltpu.VMEM((groups, ch_dev, MOS_ROWS, LANES), jnp.float32),
            pltpu.VMEM((groups - 1, ch_dev, MOS_ROWS, LANES), jnp.float32),
            pltpu.VMEM((groups - 1, ch_dev, MOS_ROWS, LANES), jnp.float32),
            pltpu.VMEM((tiles, ch_dev, tile_rows, LANES), jnp.float32),
            pltpu.VMEM((SLOTS, depth, beams, side, side), jnp.float32),
            pltpu.VMEM((beams, side, side), jnp.float32),
            pltpu.VMEM((depth, beams, PAD + side + PAD, side), jnp.float32),
            pltpu.VMEM((groups * beams, tile_rows, LANES), jnp.float32),
            pltpu.VMEM((tiles * ch_dev, tile_rows, LANES), jnp.float32),
            dma((SLOTS,)),
            dma((4,)),
            dma((steps, groups)),
            dma((steps, groups)),
            dma((groups,)),
            dma((groups,)),
            dma((tiles - 1,)),
            dma((tiles - 1,)),
            dma((tiles - 1,)),
            dma((tiles - 1,)),
            dma((groups - 1,)),
            dma((groups - 1,)),
        ],
        compiler_params=pltpu.CompilerParams(
            collective_id=0, has_side_effects=True, vmem_limit_bytes=56 << 20
        ),
        name="exchange",
    )(offsets, beam_weight, images, flags, logs)


def solve_cubic(normal_matrix, right_side):
    factor = {}
    for outer in range(4):
        for inner in range(outer + 1):
            value = normal_matrix[outer, inner]
            for other in range(inner):
                value = value - factor[outer, other] * factor[inner, other]
            if outer == inner:
                factor[outer, outer] = jnp.sqrt(value)
            else:
                factor[outer, inner] = value / factor[inner, inner]
    forward = []
    for outer in range(4):
        value = right_side[outer]
        for other in range(outer):
            value = value - factor[outer, other] * forward[other]
        forward.append(value / factor[outer, outer])
    backward = [None] * 4
    for outer in range(3, -1, -1):
        value = forward[outer]
        for other in range(outer + 1, 4):
            value = value - factor[other, outer] * backward[other]
        backward[outer] = value / factor[outer, outer]
    return backward


POLYNOMIALS = (
    {0: 1.0},
    {1: 1.0},
    {0: -0.5, 2: 1.5},
    {1: -1.5, 3: 2.5},
)


def fit_kernel(regression_ref, sky_ref, flag_ref, weights_ref, out_ref, total_ref):
    channels, rows, _ = sky_ref.shape

    def position(channel):
        return (2.0 * channel.astype(jnp.float32) + 1.0) * (1.0 / channels) - 1.0

    def gather(channel, carry):
        powers, rights = list(carry[:7]), list(carry[7:])
        x = position(channel)
        open_sky = 1.0 - flag_ref[channel].astype(jnp.float32)
        total = weights_ref[channel]
        sky = open_sky * sky_ref[channel] / total
        total_ref[channel] = sky
        chosen = regression_ref[channel].astype(jnp.float32)
        weight = total * (chosen * open_sky + 0.01)
        right = weight * sky
        for k in range(7):
            powers[k] = powers[k] + weight
            if k < 6:
                weight = weight * x
        for k in range(4):
            rights[k] = rights[k] + right
            if k < 3:
                right = right * x
        return tuple(powers) + tuple(rights)

    zero = jnp.zeros((rows, LANES), jnp.float32)
    sums = lax.fori_loop(0, channels, gather, (zero,) * 11, unroll=4)
    powers, rights = sums[:7], sums[7:]
    normal = {}
    for outer in range(4):
        for inner in range(outer + 1):
            terms = {}
            for a, u in POLYNOMIALS[outer].items():
                for b, v in POLYNOMIALS[inner].items():
                    terms[a + b] = terms.get(a + b, 0.0) + u * v
            normal[outer, inner] = sum(v * powers[k] for k, v in terms.items())
    right_side = [sum(v * rights[k] for k, v in POLYNOMIALS[o].items()) for o in range(4)]
    fitted = solve_cubic(normal, right_side)

    def residual(channel):
        x = position(channel)
        square = x * x
        continuum = (
            fitted[0]
            + x * fitted[1]
            + (0.5 * (3.0 * square - 1.0)) * fitted[2]
            + (0.5 * (5.0 * square * x - 3.0 * x)) * fitted[3]
        )
        return total_ref[channel] - continuum

    def smooth(channel, carry):
        before, here = carry
        after = residual(channel + 1)
        out_ref[channel] = 0.25 * before + 0.5 * here + 0.25 * after
        return here, after

    before, here = lax.fori_loop(
        0, channels - 1, smooth, (zero, residual(jnp.int32(0))), unroll=3
    )
    out_ref[channels - 1] = 0.25 * before + 0.5 * here


def fit(regression, sky, flags, total):
    smem = pl.BlockSpec(memory_space=pltpu.SMEM)
    vmem = pl.BlockSpec(memory_space=pltpu.VMEM)
    return pl.pallas_call(
        fit_kernel,
        in_specs=[smem, vmem, vmem, vmem],
        out_specs=vmem,
        out_shape=jax.ShapeDtypeStruct(sky.shape, jnp.float32),
        scratch_shapes=[pltpu.VMEM(sky.shape, jnp.float32)],
        compiler_params=pltpu.CompilerParams(vmem_limit_bytes=48 << 20),
        name="fit",
    )(regression, sky, flags, total)


def local(
    images, beam_weight, offsets, rejected_indicator, regression_indicator, *, groups, tiles
):
    ch_dev = images.shape[0]
    tile_rows = MOS_ROWS // tiles
    where = (lax.axis_index("chan") * tile_rows).astype(jnp.int32)[None]
    logs = log_tiles(where, offsets, beam_weight, groups, tile_rows)
    flags = rejected_indicator.reshape(ch_dev, tiles, tile_rows, rejected_indicator.shape[2])
    sky, flags, total = exchange(offsets, beam_weight, images, flags, logs, groups, tiles)
    return fit(regression_indicator, sky, flags, total)


def solution(mesh):
    in_specs = (
        P("chan", "beam", None, None),
        P("beam", None, None),
        P("beam", None),
        P("chan", None, "beam"),
        P(),
    )
    out_specs = P(None, "chan", "beam")
    body = functools.partial(local, groups=mesh.shape["beam"], tiles=mesh.shape["chan"])
    return jax.shard_map(body, mesh=mesh, in_specs=in_specs, out_specs=out_specs, check_vma=False)
```

```python
import functools

import jax
import jax.numpy as jnp
from jax import lax
from jax.experimental import pallas as pl
from jax.experimental.pallas import tpu as pltpu
from jax.sharding import PartitionSpec as P

MOS_ROWS = 192
MOS_COLS = 512
GRID = 6
JITTER = 16
LANES = 128
OUTSIDE = -1.0e4
PAD = 40
SLOTS = 3
MESH = pl.DeviceIdType.MESH


def start_range(position, span):
    if position == 0:
        return 0, 0
    if position == GRID - 1:
        return span, span
    middle = position * span // (GRID - 1)
    return max(0, middle - JITTER), min(span, middle + JITTER)


def covered_rows(group, beams_each, side, block):
    first, last = MOS_ROWS, 0
    for beam in range(group * beams_each, (group + 1) * beams_each):
        low, high = start_range(beam % GRID, MOS_COLS - side)
        if high + side <= block * LANES or low >= (block + 1) * LANES:
            continue
        low, high = start_range(beam // GRID, MOS_ROWS - side)
        first, last = min(first, low), max(last, high + side)
    return first // 8 * 8, min(MOS_ROWS, -(-last // 8) * 8)


def reaching(group, beams_each, side, block):
    found = []
    for place in range(beams_each):
        low, high = start_range((group * beams_each + place) % GRID, MOS_COLS - side)
        if high + side > block * LANES and low < (block + 1) * LANES:
            found.append(place)
    return found


def foldable(group, beams_each, side, block, upward):
    if block == group:
        return False
    for place in reaching(group, beams_each, side, block):
        beam = group * beams_each + place
        low, high = start_range(beam // GRID, MOS_ROWS - side)
        left, right = start_range(beam % GRID, MOS_COLS - side)
        if upward and high > 0 and right + side - block * LANES > LANES // 2:
            return False
        if not upward and low < MOS_ROWS - side and left - block * LANES < LANES // 2:
            return False
    return True


def tiles_kernel(where_ref, offsets_ref, weight_ref, tiles_ref, plane_ref):
    blocks, beams, tile_rows, _ = tiles_ref.shape
    side = weight_ref.shape[1]
    piece = 64
    lane = lax.broadcasted_iota(jnp.int32, (piece, LANES), 1)

    def spread(beam, carry):
        row, col = offsets_ref[beam, 0], offsets_ref[beam, 1]
        block, shift = lax.shift_right_logical(col, 7), jnp.bitwise_and(col, LANES - 1)
        plane_ref[...] = jnp.full(plane_ref.shape, OUTSIDE, jnp.float32)

        def part(index, inner):
            start = pl.multiple_of(index * piece, piece)
            value = jnp.log(weight_ref[beam, pl.ds(start, piece), :])
            value = pltpu.roll(value, shift, 1)
            plane_ref[block, pl.ds(row + start, piece), :] = jnp.where(
                lane >= shift, value, OUTSIDE
            )

            @pl.when(block < blocks - 1)
            def _():
                plane_ref[block + 1, pl.ds(row + start, piece), :] = jnp.where(
                    lane < shift, value, OUTSIDE
                )

            return inner

        lax.fori_loop(0, side // piece, part, 0)
        tiles_ref[:, beam, :, :] = plane_ref[:, pl.ds(where_ref[0], tile_rows), :]
        return carry

    lax.fori_loop(0, beams, spread, 0)


def log_tiles(where, offsets, beam_weight, blocks, tile_rows):
    beams = beam_weight.shape[0]
    smem = pl.BlockSpec(memory_space=pltpu.SMEM)
    vmem = pl.BlockSpec(memory_space=pltpu.VMEM)
    return pl.pallas_call(
        tiles_kernel,
        in_specs=[smem, smem, vmem],
        out_specs=vmem,
        out_shape=jax.ShapeDtypeStruct((blocks, beams, tile_rows, LANES), jnp.float32),
        scratch_shapes=[pltpu.VMEM((blocks, MOS_ROWS, LANES), jnp.float32)],
        name="log_tiles",
    )(where, offsets, beam_weight)


def exchange_kernel(
    offsets_ref,
    weight_ref,
    image_ref,
    flags_ref,
    logs_ref,
    sky_out,
    flag_out,
    total_out,
    own,
    up,
    down,
    rowed,
    fetched,
    own_logs,
    padded,
    arrived,
    total,
    own_sem,
    keep_sem,
    up_recv,
    down_recv,
    up_send,
    down_send,
    sky_send,
    sky_recv,
    flag_send,
    flag_recv,
    log_send,
    log_recv,
    *,
    groups,
    tiles,
    depth,
    reach_up,
    reach_down,
    fold_up,
    fold_down,
    slope,
):
    group = lax.axis_index("beam")
    tile = lax.axis_index("chan")
    ch_dev = image_ref.shape[0]
    side = weight_ref.shape[1]
    tile_rows = flags_ref.shape[2]
    beams = logs_ref.shape[1]
    steps = ch_dev // depth
    run = tiles * depth

    others = [lax.rem(tile + k, tiles) for k in range(1, tiles)]
    columns = [lax.rem(group + k, groups) for k in range(1, groups)]

    barrier = pltpu.get_barrier_semaphore()
    for other in others:
        pl.semaphore_signal(barrier, inc=1, device_id={"chan": other}, device_id_type=MESH)
    for other in columns:
        pl.semaphore_signal(barrier, inc=1, device_id={"beam": other}, device_id_type=MESH)

    def load(step):
        slot = lax.rem(step, SLOTS)
        return pltpu.make_async_copy(
            image_ref.at[pl.ds(step * depth, depth)], fetched.at[slot], own_sem.at[slot]
        )

    for step in range(min(SLOTS, steps)):
        load(step).start()
    mine = pl.ds(tile * ch_dev, ch_dev)
    kept = [
        pltpu.make_async_copy(flags_ref.at[:, tile], flag_out.at[mine], keep_sem.at[0]),
        pltpu.make_async_copy(
            logs_ref.at[group], arrived.at[pl.ds(group * beams, beams)], keep_sem.at[1]
        ),
    ]
    for copy in kept:
        copy.start()
    pl.semaphore_wait(barrier, len(others) + len(columns))

    def log_copy(source, k, beam):
        return pltpu.make_async_remote_copy(
            src_ref=logs_ref.at[(source + k) % groups, beam],
            dst_ref=arrived.at[source * beams + beam],
            send_sem=log_send.at[k - 1],
            recv_sem=log_recv.at[k - 1],
            device_id={"beam": (source + k) % groups},
            device_id_type=MESH,
        )

    small = []
    for k, other in enumerate(others):
        small.append(
            pltpu.make_async_remote_copy(
                src_ref=flags_ref.at[:, other],
                dst_ref=flag_out.at[mine],
                send_sem=flag_send.at[k],
                recv_sem=flag_recv.at[k],
                device_id={"chan": other},
                device_id_type=MESH,
            )
        )
    for copy in small:
        copy.start()

    own_logs[...] = jnp.log(weight_ref[...])
    padded[...] = jnp.zeros(padded.shape, jnp.float32)
    lane = lax.broadcasted_iota(jnp.int32, (1, LANES), 1)

    def place(z, step):
        load(step).wait()
        slot = lax.rem(step, SLOTS)
        exponent = 1.0 + slope * (tile * ch_dev + step * depth).astype(jnp.float32)

        def weigh(beam, carry):
            logs = own_logs[beam]
            response = jnp.exp(exponent * logs)
            ratio = jnp.exp(slope * logs)
            for channel in range(depth):
                padded[channel, beam, PAD : PAD + side, :] = (
                    fetched[slot, channel, beam] * response
                )
                response = response * ratio
            return carry

        lax.fori_loop(0, beams, weigh, 0)

        @pl.when(step + SLOTS < steps)
        def _():
            load(step + SLOTS).start()

        span = pl.ds(step * depth, depth)
        own[:, span] = jnp.zeros((groups, depth, MOS_ROWS, LANES), jnp.float32)
        for beam in range(beams):
            place_row, place_col = divmod(z * beams + beam, GRID)
            low, high = start_range(place_row, MOS_ROWS - side)
            first, last = low // 8 * 8, -(-(high + side) // 8) * 8
            row = jnp.clip(offsets_ref[beam, 0], low, high)
            low, high = start_range(place_col, MOS_COLS - side)
            block = low // LANES
            values = [
                padded[channel, beam, pl.ds(PAD + first - row, last - first), :]
                for channel in range(depth)
            ]
            if low == high and low % LANES == 0:
                for channel, value in enumerate(values):
                    own[block, step * depth + channel, first:last, :] += value
                continue
            shift = jnp.clip(offsets_ref[beam, 1], low, high) - block * LANES
            values = [pltpu.roll(value, shift, 1) for value in values]
            for target, inside in ((block, lane >= shift), (block + 1, lane < shift)):
                for channel, value in enumerate(values):
                    own[target, step * depth + channel, first:last, :] += jnp.where(
                        inside, value, 0.0
                    )

    def add_weights(z, step):
        start = step * run
        exponent = 1.0 + slope * start.astype(jnp.float32)
        piece = 8 if tile_rows % 8 == 0 else tile_rows
        for part in range(tile_rows // piece):
            rows = pl.ds(part * piece, piece)
            sums = [jnp.zeros((piece, LANES), jnp.float32)] * run
            for source in range(groups):
                for beam in reaching(source, beams, side, z):
                    logs = arrived[source * beams + beam, rows, :]
                    value = jnp.exp((2.0 * exponent) * logs)
                    ratio = jnp.exp((2.0 * slope) * logs)
                    for k in range(run):
                        sums[k] = sums[k] + value
                        if k < run - 1:
                            value = value * ratio
            for k in range(run):
                total[start + k, rows, :] = sums[k]

    def unfold_up(z, block, span):
        last = reach_up[z - 1, block]
        if z != 1 or block not in fold_up:
            return last
        half = last - side
        both = up[block - 1, span, side:last, :]
        up[block - 1, span, side:last, :] = jnp.where(lane < LANES // 2, both, 0.0)
        up[block - 1, span, last : last + half, :] = pltpu.roll(
            jnp.where(lane < LANES // 2, 0.0, both), LANES // 2, 2
        )
        return last + half

    def unfold_down(z, block, span):
        first, edge = reach_down[z + 1, block], MOS_ROWS - side
        if z != groups - 2 or block not in fold_down:
            return first
        both = down[block, span, first:edge, :]
        down[block, span, first:edge, :] = jnp.where(lane < LANES // 2, 0.0, both)
        down[block, span, 2 * first - edge : first, :] = pltpu.roll(
            jnp.where(lane < LANES // 2, both, 0.0), LANES // 2, 2
        )
        return 2 * first - edge

    def up_copy(z, block, step):
        span, rows = pl.ds(step * depth, depth), pl.ds(0, reach_up[z, block])
        source = own.at[block, span, rows] if z == 0 else up.at[block - 1, span, rows]
        return pltpu.make_async_remote_copy(
            src_ref=source,
            dst_ref=up.at[block - 1, span, rows],
            send_sem=up_send.at[block],
            recv_sem=up_recv.at[step, block],
            device_id={"beam": z + 1},
            device_id_type=MESH,
        )

    def down_copy(z, block, step):
        first = reach_down[z, block]
        span, rows = pl.ds(step * depth, depth), pl.ds(first, MOS_ROWS - first)
        source = own.at[block, span, rows] if z == groups - 1 else down.at[block, span, rows]
        return pltpu.make_async_remote_copy(
            src_ref=source,
            dst_ref=down.at[block, span, rows],
            send_sem=down_send.at[block],
            recv_sem=down_recv.at[step, block],
            device_id={"beam": z - 1},
            device_id_type=MESH,
        )

    def sky_copy(k, other, span):
        return pltpu.make_async_remote_copy(
            src_ref=rowed.at[other, span],
            dst_ref=sky_out.at[pl.ds(tile * ch_dev + span.start, span.size)],
            send_sem=sky_send.at[k],
            recv_sem=sky_recv.at[k],
            device_id={"chan": other},
            device_id_type=MESH,
        )

    for z in range(groups):

        @pl.when(group == z)
        def _(z=z):
            for k in range(1, groups):
                for beam in reaching(z, beams, side, (z + k) % groups):
                    log_copy(z, k, beam).start()
            lower = 2 * z < groups
            up_lag, down_lag = (0, 2) if lower else (2, 0)
            last_lag = 6 if z in (0, groups - 1) else 3

            def pass_up(step):
                span = pl.ds(step * depth, depth)
                for block in range(groups - 1, z, -1):
                    if z > 0:
                        up_copy(z - 1, block, step).wait_recv()
                        old, new = unfold_up(z, block, span), reach_up[z, block]
                        up[block - 1, span, 0:old, :] += own[block, span, 0:old, :]
                        if new > old:
                            up[block - 1, span, old:new, :] = own[block, span, old:new, :]
                    elif block in fold_up:
                        last = reach_up[z, block]
                        own[block, span, side:last, :] += pltpu.roll(
                            own[block, span, last : 2 * last - side, :], LANES // 2, 2
                        )
                    up_copy(z, block, step).start()

            def pass_down(step):
                span = pl.ds(step * depth, depth)
                for block in range(z):
                    if z < groups - 1:
                        down_copy(z + 1, block, step).wait_recv()
                        old, new = unfold_down(z, block, span), reach_down[z, block]
                        down[block, span, old:, :] += own[block, span, old:, :]
                        if new < old:
                            down[block, span, new:old, :] = own[block, span, new:old, :]
                    elif block in fold_down:
                        first, edge = reach_down[z, block], MOS_ROWS - side
                        own[block, span, first:edge, :] += pltpu.roll(
                            own[block, span, 2 * first - edge : first, :], LANES // 2, 2
                        )
                    down_copy(z, block, step).start()

            def finish(step):
                span = pl.ds(step * depth, depth)
                if z > 0:
                    up_copy(z - 1, z, step).wait_recv()
                    old = unfold_up(z, z, span)
                    own[z, span, 0:old, :] += up[z - 1, span, 0:old, :]
                if z < groups - 1:
                    down_copy(z + 1, z, step).wait_recv()
                    old = unfold_down(z, z, span)
                    own[z, span, old:, :] += down[z, span, old:, :]
                for index in range(tiles):
                    rowed[index, span, :, :] = own[
                        z, span, index * tile_rows : (index + 1) * tile_rows, :
                    ]
                for k, other in enumerate(others):
                    sky_copy(k, other, span).start()

            def work(turn, carry):
                @pl.when(turn < steps)
                def _():
                    place(z, turn)

                for lag, act in ((up_lag, pass_up), (down_lag, pass_down), (last_lag, finish)):

                    @pl.when(jnp.logical_and(turn >= lag, turn < steps + lag))
                    def _(lag=lag, act=act):
                        act(turn - lag)

                @pl.when(turn == 1)
                def _():
                    kept[1].wait()
                    for k in range(1, groups):
                        count = len(reaching(z, beams, side, (z + k) % groups))
                        ref = arrived.at[pl.ds(0, count)]
                        if count:
                            pltpu.make_async_copy(ref, ref, log_send.at[k - 1]).wait()
                        count = len(reaching((z - k) % groups, beams, side, z))
                        ref = arrived.at[pl.ds(0, count)]
                        if count:
                            pltpu.make_async_copy(ref, ref, log_recv.at[k - 1]).wait()

                @pl.when(jnp.logical_and(turn >= 1, turn < steps + 1))
                def _():
                    add_weights(z, turn - 1)

                return carry

            lax.fori_loop(0, steps + last_lag, work, 0)
            for block in range(z + 1, groups):
                ref = up.at[block - 1, :, pl.ds(0, reach_up[z, block])]
                pltpu.make_async_copy(ref, ref, up_send.at[block]).wait()
            for block in range(z):
                first = reach_down[z, block]
                ref = down.at[block, :, pl.ds(first, MOS_ROWS - first)]
                pltpu.make_async_copy(ref, ref, down_send.at[block]).wait()

    last = [
        pltpu.make_async_copy(rowed.at[tile], sky_out.at[mine], keep_sem.at[2]),
        pltpu.make_async_copy(total, total_out, keep_sem.at[3]),
        kept[0],
    ]
    for copy in last[:2]:
        copy.start()
    for copy in small:
        copy.wait()
    for k, other in enumerate(others):
        sky_copy(k, other, pl.ds(0, ch_dev)).wait()
    for copy in last:
        copy.wait()


def exchange(offsets, beam_weight, images, flags, logs, groups, tiles):
    ch_dev, _, side, _ = images.shape
    tile_rows = flags.shape[2]
    beams = logs.shape[1]
    depth = 2
    steps = ch_dev // depth
    reach_up, reach_down = {}, {}
    for block in range(groups):
        rows = [covered_rows(group, beams, side, block) for group in range(groups)]
        for z in range(groups):
            reach_up[z, block] = max(high for _, high in rows[: z + 1])
            reach_down[z, block] = min(low for low, _ in rows[z:])
    fold_up, fold_down = [], []
    edge = MOS_ROWS - side
    for block in range(groups):
        extra = reach_up[0, block] - side
        if extra > 0 and extra % 16 == 0 and foldable(0, beams, side, block, True):
            fold_up.append(block)
            reach_up[0, block] = side + extra // 2
        extra = edge - reach_down[groups - 1, block]
        if extra > 0 and extra % 16 == 0 and foldable(groups - 1, beams, side, block, False):
            fold_down.append(block)
            reach_down[groups - 1, block] = edge - extra // 2
    dma = pltpu.SemaphoreType.DMA
    any_space = pl.BlockSpec(memory_space=pl.ANY)
    return pl.pallas_call(
        functools.partial(
            exchange_kernel,
            groups=groups,
            tiles=tiles,
            depth=depth,
            reach_up=reach_up,
            reach_down=reach_down,
            fold_up=fold_up,
            fold_down=fold_down,
            slope=0.5 / (tiles * ch_dev - 1),
        ),
        in_specs=[
            pl.BlockSpec(memory_space=pltpu.SMEM),
            pl.BlockSpec(memory_space=pltpu.VMEM),
            any_space,
            any_space,
            any_space,
        ],
        out_specs=[any_space] * 3,
        out_shape=[
            jax.ShapeDtypeStruct((tiles * ch_dev, tile_rows, LANES), jnp.float32),
            jax.ShapeDtypeStruct((tiles * ch_dev, tile_rows, LANES), jnp.int32),
            jax.ShapeDtypeStruct((tiles * ch_dev, tile_rows, LANES), jnp.float32),
        ],
        scratch_shapes=[
            pltpu.VMEM((groups, ch_dev, MOS_ROWS, LANES), jnp.float32),
            pltpu.VMEM((groups - 1, ch_dev, MOS_ROWS, LANES), jnp.float32),
            pltpu.VMEM((groups - 1, ch_dev, MOS_ROWS, LANES), jnp.float32),
            pltpu.VMEM((tiles, ch_dev, tile_rows, LANES), jnp.float32),
            pltpu.VMEM((SLOTS, depth, beams, side, side), jnp.float32),
            pltpu.VMEM((beams, side, side), jnp.float32),
            pltpu.VMEM((depth, beams, PAD + side + PAD, side), jnp.float32),
            pltpu.VMEM((groups * beams, tile_rows, LANES), jnp.float32),
            pltpu.VMEM((tiles * ch_dev, tile_rows, LANES), jnp.float32),
            dma((SLOTS,)),
            dma((4,)),
            dma((steps, groups)),
            dma((steps, groups)),
            dma((groups,)),
            dma((groups,)),
            dma((tiles - 1,)),
            dma((tiles - 1,)),
            dma((tiles - 1,)),
            dma((tiles - 1,)),
            dma((groups - 1,)),
            dma((groups - 1,)),
        ],
        compiler_params=pltpu.CompilerParams(
            collective_id=0, has_side_effects=True, vmem_limit_bytes=56 << 20
        ),
        name="exchange",
    )(offsets, beam_weight, images, flags, logs)


def solve_cubic(normal_matrix, right_side):
    factor = {}
    for outer in range(4):
        for inner in range(outer + 1):
            value = normal_matrix[outer, inner]
            for other in range(inner):
                value = value - factor[outer, other] * factor[inner, other]
            if outer == inner:
                factor[outer, outer] = jnp.sqrt(value)
            else:
                factor[outer, inner] = value / factor[inner, inner]
    forward = []
    for outer in range(4):
        value = right_side[outer]
        for other in range(outer):
            value = value - factor[outer, other] * forward[other]
        forward.append(value / factor[outer, outer])
    backward = [None] * 4
    for outer in range(3, -1, -1):
        value = forward[outer]
        for other in range(outer + 1, 4):
            value = value - factor[other, outer] * backward[other]
        backward[outer] = value / factor[outer, outer]
    return backward


POLYNOMIALS = (
    {0: 1.0},
    {1: 1.0},
    {0: -0.5, 2: 1.5},
    {1: -1.5, 3: 2.5},
)


def fit_kernel(
    regression_ref,
    sky_in,
    flag_in,
    weights_in,
    result_ref,
    sky_ref,
    flag_ref,
    weights_ref,
    out_ref,
    total_ref,
    in_sem,
    out_sem,
):
    channels, rows, _ = sky_ref.shape
    chunks = out_sem.shape[0]
    size = channels // chunks
    pairs = ((sky_in, sky_ref), (flag_in, flag_ref), (weights_in, weights_ref))
    incoming = [
        [
            pltpu.make_async_copy(
                source.at[pl.ds(i * size, size)],
                target.at[pl.ds(i * size, size)],
                in_sem.at[k, i],
            )
            for k, (source, target) in enumerate(pairs)
        ]
        for i in range(chunks)
    ]
    for copies in incoming:
        for copy in copies:
            copy.start()

    def position(channel):
        return (2.0 * channel.astype(jnp.float32) + 1.0) * (1.0 / channels) - 1.0

    def gather(channel, carry):
        powers, rights = list(carry[:7]), list(carry[7:])
        x = position(channel)
        open_sky = 1.0 - flag_ref[channel].astype(jnp.float32)
        total = weights_ref[channel]
        sky = open_sky * sky_ref[channel] / total
        total_ref[channel] = sky
        chosen = regression_ref[channel].astype(jnp.float32)
        weight = total * (chosen * open_sky + 0.01)
        right = weight * sky
        for k in range(7):
            powers[k] = powers[k] + weight
            if k < 6:
                weight = weight * x
        for k in range(4):
            rights[k] = rights[k] + right
            if k < 3:
                right = right * x
        return tuple(powers) + tuple(rights)

    zero = jnp.zeros((rows, LANES), jnp.float32)
    sums = (zero,) * 11
    for i, copies in enumerate(incoming):
        for copy in copies:
            copy.wait()
        sums = lax.fori_loop(i * size, (i + 1) * size, gather, sums, unroll=4)
    powers, rights = sums[:7], sums[7:]
    normal = {}
    for outer in range(4):
        for inner in range(outer + 1):
            terms = {}
            for a, u in POLYNOMIALS[outer].items():
                for b, v in POLYNOMIALS[inner].items():
                    terms[a + b] = terms.get(a + b, 0.0) + u * v
            normal[outer, inner] = sum(v * powers[k] for k, v in terms.items())
    right_side = [sum(v * rights[k] for k, v in POLYNOMIALS[o].items()) for o in range(4)]
    fitted = solve_cubic(normal, right_side)

    def residual(channel):
        x = position(channel)
        square = x * x
        continuum = (
            fitted[0]
            + x * fitted[1]
            + (0.5 * (3.0 * square - 1.0)) * fitted[2]
            + (0.5 * (5.0 * square * x - 3.0 * x)) * fitted[3]
        )
        return total_ref[channel] - continuum

    def smooth(channel, carry):
        before, here = carry
        after = residual(channel + 1)
        out_ref[channel] = 0.25 * before + 0.5 * here + 0.25 * after
        return here, after

    state = (zero, residual(jnp.int32(0)))
    outgoing = []
    for i in range(chunks):
        final = i == chunks - 1
        stop = channels - 1 if final else (i + 1) * size
        state = lax.fori_loop(i * size, stop, smooth, state, unroll=1 if final else 4)
        if final:
            out_ref[channels - 1] = 0.25 * state[0] + 0.5 * state[1]
        span = pl.ds(i * size, size)
        outgoing.append(
            pltpu.make_async_copy(out_ref.at[span], result_ref.at[span], out_sem.at[i])
        )
        outgoing[-1].start()
    for copy in outgoing:
        copy.wait()


def fit(regression, sky, flags, total):
    smem = pl.BlockSpec(memory_space=pltpu.SMEM)
    any_space = pl.BlockSpec(memory_space=pl.ANY)
    chunks = 8
    held = pltpu.VMEM(sky.shape, jnp.float32)
    return pl.pallas_call(
        fit_kernel,
        in_specs=[smem, any_space, any_space, any_space],
        out_specs=any_space,
        out_shape=jax.ShapeDtypeStruct(sky.shape, jnp.float32),
        scratch_shapes=[
            held,
            pltpu.VMEM(sky.shape, jnp.int32),
            held,
            held,
            held,
            pltpu.SemaphoreType.DMA((3, chunks)),
            pltpu.SemaphoreType.DMA((chunks,)),
        ],
        compiler_params=pltpu.CompilerParams(vmem_limit_bytes=48 << 20),
        name="fit",
    )(regression, sky, flags, total)


def local(
    images, beam_weight, offsets, rejected_indicator, regression_indicator, *, groups, tiles
):
    ch_dev = images.shape[0]
    tile_rows = MOS_ROWS // tiles
    where = (lax.axis_index("chan") * tile_rows).astype(jnp.int32)[None]
    logs = log_tiles(where, offsets, beam_weight, groups, tile_rows)
    flags = rejected_indicator.reshape(ch_dev, tiles, tile_rows, rejected_indicator.shape[2])
    sky, flags, total = exchange(offsets, beam_weight, images, flags, logs, groups, tiles)
    return fit(regression_indicator, sky, flags, total)


def solution(mesh):
    in_specs = (
        P("chan", "beam", None, None),
        P("beam", None, None),
        P("beam", None),
        P("chan", None, "beam"),
        P(),
    )
    out_specs = P(None, "chan", "beam")
    body = functools.partial(local, groups=mesh.shape["beam"], tiles=mesh.shape["chan"])
    return jax.shard_map(body, mesh=mesh, in_specs=in_specs, out_specs=out_specs, check_vma=False)
```
